32 devices in a mesh: mode: 2 (over x), slab: 16 (over z, y, core).
Axes of the slice: x: 2, y: 2, z: 4, core: 2. Of those that a mesh axis runs over, the one named last changes fastest.
Arguments:
- log_cond: float32 [64, 128, 128], P('slab'), may hold values from -1 to 1
- head_slope: float32 [64, 128, 128], P('slab'), may hold values from -6 to 6
- modes: bfloat16 [64, 64, 128, 128], P('mode', 'slab'), may hold values from -6 to 6
- obs_cells: int32 [16384], P('slab'), may hold values from 0 to 65535
- obs_var: float32 [16384], P('slab'), may hold values from 0.2 to 2
- misfit: float32 [16384, 16], P('slab'), may hold values from -24 to 24
- base_fields: bfloat16 [16, 64, 128, 128], P(None, 'slab', 'mode'), may hold values from -6 to 6
Outputs:
- fields: float32 [16, 64, 128, 128], P(None, 'slab', 'mode')
The draws below stay inside these ranges and needn't reach their ends.
Inputs may be any that keep to these rules, and one draw needn't show every extreme that they name: `obs_cells`: entry o names a cell of the planes (o // 1024) * 4 to (o // 1024 + 1) * 4 - 1, counted from the first of them: value c stands for plane (o // 1024) * 4 + c // 16384, first horizontal index (c // 128) % 128, second c % 128; cells may repeat.
All inputs are finite; a program needn't handle non-finite values.
Results may differ from the reference program's by a relative error of at most 0.0003.
Values may be sent and summed in bfloat16 or wider, within the bound.
A program may use at most 128 MiB of HBM per device.

```python
import math
import jax
import jax.numpy as jnp
from jax import lax

NX = 128
NY = 128
CZ = 4
MODES = 64
FIELDS = 16
ITERS = 3
OBS_SLAB = 1024
OBS = 16384
NZ = 64


def place_ends(values, rng, smallest, high):
    extent = values.shape
    place = [jax.random.randint(jax.random.fold_in(rng, axis), (), 0, extent[axis]) for axis in range(len(extent))]
    values = values.at[tuple(place)].set(smallest)
    longest = extent.index(max(extent))
    place[longest] = (place[longest] + 1) % extent[longest]
    return values.at[tuple(place)].set(high)


def shard_levels(rng, extent, pieces, smallest, high):
    level = 1.0
    for dim, parts in pieces:
        heights = jax.random.uniform(jax.random.fold_in(jax.random.fold_in(rng, 6), dim), (parts,), jnp.float32, smallest / len(pieces), high / len(pieces))
        level = level * jnp.repeat(jnp.exp(heights), extent[dim] // parts).reshape((-1,) + (1,) * (len(extent) - 1 - dim))
    return level


def normal_values(own_key, shape, deviation, limit, cuts=(), kind=jnp.bfloat16):
    level = shard_levels(own_key, shape, cuts, -0.22, 0.18) if cuts else 1.0
    values = jax.random.normal(own_key, shape, jnp.float32) * deviation * level
    return jnp.minimum(jnp.maximum(values, -limit), limit).astype(kind)


def setup_inputs(seed: int = 0) -> dict:
    keys = jax.random.split(jax.random.key(seed), 8)
    return {
        "log_cond": jnp.clip(jax.random.uniform(keys[0], (NZ, NX, NY), jnp.float32, -1.0, 1.0) * shard_levels(keys[0], (NZ, NX, NY), ((0, 16),), -0.4, 0.0), -1.0, 1.0),
        "head_slope": normal_values(keys[1], (NZ, NX, NY), 1.0, 6.0, ((0, 16),), jnp.float32),
        "modes": normal_values(keys[2], (MODES, NZ, NX, NY), 1.0, 6.0, ((0, 2), (1, 16))),
        "obs_cells": place_ends(jax.random.randint(keys[3], (OBS,), 0, CZ * NX * NY), jax.random.fold_in(keys[3], 1), 0, (CZ * NX * NY) - 1).astype(jnp.int32),
        "obs_var": jnp.clip(jnp.exp(math.log(2.0) - 2.3025851 * jax.random.uniform(keys[4], (OBS,), jnp.float32) ** shard_levels(keys[4], (OBS,), ((0, 16),), -0.2, 0.2)), 0.2, 2.0),
        "misfit": normal_values(keys[5], (OBS, FIELDS), 4.0, 24.0, ((0, 16),), jnp.float32),
        "base_fields": normal_values(keys[6], (FIELDS, NZ, NX, NY), 1.0, 6.0, ((1, 16), (2, 2))),
    }


STORAGE = 0.05

def sweep_weights(count):
    order = []
    low, high = (0, count - 1)
    while low <= high:
        order.append(low)
        if high != low:
            order.append(high)
        low += 1
        high -= 1
    return [1.0 / (1.15 + 0.85 * math.cos((2 * i + 1) * math.pi / (2 * count))) for i in order]

def coefficients(cond_ext):
    padded = jnp.pad(cond_ext, ((0, 0), (1, 1), (1, 1)), mode='edge')
    centre = padded[1:-1, 1:-1, 1:-1]

    def harmonic(other):
        return 2.0 * centre * other / (centre + other)
    lower = harmonic(padded[:-2, 1:-1, 1:-1])
    upper = harmonic(padded[2:, 1:-1, 1:-1])
    west = harmonic(padded[1:-1, :-2, 1:-1])
    east = harmonic(padded[1:-1, 2:, 1:-1])
    south = harmonic(padded[1:-1, 1:-1, :-2])
    north = harmonic(padded[1:-1, 1:-1, 2:])
    diag = STORAGE + lower + upper + west + east + south + north
    return (lower, upper, west, east, south, north, diag)

def relax(u_ext, source, coeffs, weight):
    lower, upper, west, east, south, north, diag = coeffs
    core = u_ext[:, 1:-1]
    px = jnp.pad(core, ((0, 0), (0, 0), (1, 1), (0, 0)))
    py = jnp.pad(core, ((0, 0), (0, 0), (0, 0), (1, 1)))
    beside = lower * u_ext[:, :-2] + upper * u_ext[:, 2:] + west * px[:, :, :-2] + east * px[:, :, 2:] + south * py[..., :-2] + north * py[..., 2:]
    return core + weight * (source - (diag * core - beside)) / diag

def reference(log_cond, head_slope, modes, obs_cells, obs_var, misfit, base_fields):
    cond = jnp.exp(log_cond)
    coeffs = coefficients(jnp.pad(cond, ((1, 1), (0, 0), (0, 0)), mode='edge'))
    weights = sweep_weights(ITERS)
    positions = jnp.arange(OBS, dtype=jnp.int32) // OBS_SLAB * (CZ * NX * NY) + obs_cells.astype(jnp.int32)

    def respond(mode):
        source = (head_slope * cond * mode.astype(jnp.float32))[None]
        head = jnp.zeros_like(source)
        for weight in weights:
            head = relax(jnp.pad(head, ((0, 0), (1, 1), (0, 0), (0, 0))), source, coeffs, weight)
        return jnp.take(head.reshape(-1), positions)
    response = lax.map(respond, modes)
    scaled = response / obs_var[None, :]
    gram = jnp.dot(scaled, response.T, precision=lax.Precision.HIGHEST) + jnp.eye(response.shape[0], dtype=jnp.float32)
    rhs = jnp.dot(scaled, misfit, precision=lax.Precision.HIGHEST)
    factor = jnp.linalg.cholesky(gram)
    coef = jax.scipy.linalg.cho_solve((factor, True), rhs)

    def plane(level):
        layer = lax.dynamic_index_in_dim(modes, level, 1, keepdims=False)
        layer = layer.reshape(layer.shape[0], -1).astype(jnp.float32)
        return jnp.dot(coef.T, layer, precision=lax.Precision.HIGHEST).reshape(coef.shape[1], NX, NY)
    update = lax.map(plane, jnp.arange(NZ, dtype=jnp.int32))
    return base_fields.astype(jnp.float32) + jnp.transpose(update, (1, 0, 2, 3))
```

```python
import functools
import math

import jax
import jax.numpy as jnp
from jax import lax
from jax.experimental import pallas as pl
from jax.experimental.pallas import tpu as pltpu
from jax.sharding import PartitionSpec as P

ITERS = 3
STORAGE = 0.05
REACH = ITERS - 1
MIB = 1 << 20


def sweep_weights(count):
    order = []
    low, high = (0, count - 1)
    while low <= high:
        order.append(low)
        if high != low:
            order.append(high)
        low += 1
        high -= 1
    return [1.0 / (1.15 + 0.85 * math.cos((2 * i + 1) * math.pi / (2 * count))) for i in order]


W0, W1, W2 = sweep_weights(ITERS)
SCALE_B = W0 * W1
SCALE_A = (1.0 - W1) * W0 + W1
SELF_2 = SCALE_A / SCALE_B
SELF_3 = (1.0 - W2) / W2
SOURCE_3 = 1.0 / SCALE_B


def stencil_kernel(
    planes, width, modes_count, group, edge_ref, cells_ref, cells_b_ref, cells_a_ref,
    log_ref, slope_ref, modes_ref, own_ref, below_ref, above_ref,
    coef, gain, cond, t_ref, u_ref, r_ref,
):
    step = pl.program_id(0)
    lanes = log_ref.shape[-1]
    pad = 8
    tiles = width // 8
    stride = (planes + 2 * REACH) * width + pad
    n_ext = planes + 2 * REACH + 2

    @pl.when(step == 0)
    def _():
        cond[...] = jnp.ones_like(cond)
        for z in range(n_ext):
            cond[pl.ds(pad + z * width, width), :] = jnp.exp(log_ref[z])

        @pl.when(edge_ref[0] == 1)
        def _():
            cond[pl.ds(pad + 2 * width, width), :] = cond[pl.ds(pad + 3 * width, width), :]

        @pl.when(edge_ref[1] == 1)
        def _():
            cond[pl.ds(pad + (planes + 3) * width, width), :] = cond[
                pl.ds(pad + (planes + 2) * width, width), :
            ]

        t_ref[...] = jnp.zeros_like(t_ref)
        u_ref[...] = jnp.zeros_like(u_ref)
        rows = lax.broadcasted_iota(jnp.int32, (8, lanes), 0)
        cols = lax.broadcasted_iota(jnp.int32, (8, lanes), 1)
        first = edge_ref[0] == 1
        last = edge_ref[1] == 1
        for z in range(planes + 2 * REACH):
            def body(i, carry, z=z):
                at = pad + (z + 1) * width + i * 8
                c = cond[pl.ds(at, 8), :]

                def harmonic(other):
                    return 2.0 * c * other / (c + other)

                x = rows + i * 8
                lower = harmonic(cond[pl.ds(at - width, 8), :])
                upper = harmonic(cond[pl.ds(at + width, 8), :])
                west = harmonic(jnp.where(x == 0, c, cond[pl.ds(at - 1, 8), :]))
                east = harmonic(jnp.where(x == width - 1, c, cond[pl.ds(at + 1, 8), :]))
                south = harmonic(jnp.where(cols == 0, c, pltpu.roll(c, 1, axis=1)))
                north = harmonic(jnp.where(cols == lanes - 1, c, pltpu.roll(c, lanes - 1, axis=1)))
                inverse = 1.0 / (STORAGE + lower + upper + west + east + south + north)
                zero = jnp.zeros_like(c)
                if z < REACH:
                    upper = jnp.where(first, zero, upper)
                if z == REACH:
                    lower = jnp.where(first, zero, lower)
                if z == REACH + planes - 1:
                    upper = jnp.where(last, zero, upper)
                if z >= REACH + planes:
                    lower = jnp.where(last, zero, lower)
                here = pl.ds(i * 8, 8)
                coef[z, 0, here, :] = lower * inverse
                coef[z, 1, here, :] = upper * inverse
                coef[z, 2, here, :] = jnp.where(x == 0, zero, west * inverse)
                coef[z, 3, here, :] = jnp.where(x == width - 1, zero, east * inverse)
                coef[z, 4, here, :] = jnp.where(cols == 0, zero, south * inverse)
                coef[z, 5, here, :] = jnp.where(cols == lanes - 1, zero, north * inverse)
                if REACH <= z < REACH + planes:
                    gain[z - REACH, here, :] = (
                        (W2 * SCALE_B) * slope_ref[z - REACH, here, :] * c * inverse
                    )
                return carry

            lax.fori_loop(0, tiles, body, 0)
        for k in range(modes_count):
            r_ref[pl.ds(k * stride + stride - pad, pad), :] = jnp.zeros((pad, lanes), jnp.float32)

    for z in range(planes):
        def convert(i, carry, z=z):
            here = pl.ds(i * 16, 16)
            g = gain[z, here, :]
            for m in range(group):
                t_ref[m, pl.ds(pad + z * width + i * 16, 16), :] = g * modes_ref[
                    m, z, here, :
                ].astype(jnp.float32)
            return carry

        lax.fori_loop(0, width // 16, convert, 0)

    def beside(ref, m, at, c, terms):
        total = None
        centre = ref[m, pl.ds(at, 8), :]
        for name in terms:
            if name == 0:
                v = ref[m, pl.ds(at - width, 8), :]
            elif name == 1:
                v = ref[m, pl.ds(at + width, 8), :]
            elif name == 2:
                v = ref[m, pl.ds(at - 1, 8), :]
            elif name == 3:
                v = ref[m, pl.ds(at + 1, 8), :]
            elif name == 4:
                v = pltpu.roll(centre, 1, axis=1)
            else:
                v = pltpu.roll(centre, lanes - 1, axis=1)
            v = c[name] * v
            total = v if total is None else total + v
        return centre, total

    for z in range(-1, planes + 1):
        if z == -1:
            terms = (1,)
        elif z == planes:
            terms = (0,)
        else:
            terms = (2, 3, 4, 5) + ((0,) if z > 0 else ()) + ((1,) if z < planes - 1 else ())

        def second(i, carry, z=z, terms=terms):
            c = {n: coef[z + REACH, n, pl.ds(i * 8, 8), :] for n in terms}
            at = pad + z * width + i * 8
            put = pl.ds(pad + (z + 1) * width + i * 8, 8)
            for m in range(group):
                if 0 <= z < planes:
                    centre, total = beside(t_ref, m, at, c, terms)
                    total = total + SELF_2 * centre
                elif z == -1:
                    total = c[1] * t_ref[m, pl.ds(at + width, 8), :]
                else:
                    total = c[0] * t_ref[m, pl.ds(at - width, 8), :]
                u_ref[m, put, :] = total
            return carry

        lax.fori_loop(0, tiles, second, 0)

    for z in range(-2, planes + 2):
        if z == -2:
            terms = (1,)
        elif z == planes + 1:
            terms = (0,)
        else:
            terms = (2, 3, 4, 5) + ((0,) if z > -1 else ()) + ((1,) if z < planes else ())

        def third(i, carry, z=z, terms=terms):
            c = {n: coef[z + REACH, n, pl.ds(i * 8, 8), :] for n in terms}
            at = pad + (z + 1) * width + i * 8
            for m in range(group):
                if z == -2:
                    total = c[1] * u_ref[m, pl.ds(at + width, 8), :]
                elif z == planes + 1:
                    total = c[0] * u_ref[m, pl.ds(at - width, 8), :]
                else:
                    centre, total = beside(u_ref, m, at, c, terms)
                    total = total + SELF_3 * centre
                    if 0 <= z < planes:
                        total = total + SOURCE_3 * t_ref[m, pl.ds(pad + z * width + i * 8, 8), :]
                put = pl.multiple_of(
                    (step * group + m) * stride + (z + REACH) * width + i * 8, 8
                )
                r_ref[pl.ds(put, 8), :] = total
            return carry

        lax.fori_loop(0, tiles, third, 0)

    @pl.when(step == pl.num_programs(0) - 1)
    def _():
        cols = lax.broadcasted_iota(jnp.int32, (modes_count, lanes), 1)
        count = cells_ref.shape[0]
        zero_row = stride - pad
        shift = lanes.bit_length() - 1

        def pick(cells, out, low, high, offset):
            def block(b, carry):
                def one(i, acc):
                    cell = cells[b * lanes + i]
                    row = cell >> shift
                    lane = cell & (lanes - 1)
                    if low is not None:
                        inside = jnp.logical_and(row >= low, row < high)
                        row = jnp.where(inside, row + offset, zero_row)
                    else:
                        row = row + offset
                    v = r_ref[pl.ds(row, modes_count, stride=stride), :]
                    v = pltpu.roll(v, (i - lane) & (lanes - 1), axis=1)
                    return jnp.where(cols == i, v, acc)

                acc = lax.fori_loop(
                    0, lanes, one, jnp.zeros((modes_count, lanes), jnp.float32), unroll=8
                )
                out[:, pl.ds(pl.multiple_of(b * lanes, lanes), lanes)] = acc
                return carry

            lax.fori_loop(0, count // lanes, block, 0)

        pick(cells_ref, own_ref, None, None, REACH * width)
        pick(
            cells_b_ref, below_ref, (planes - REACH) * width, planes * width,
            (REACH - planes) * width,
        )
        pick(cells_a_ref, above_ref, 0, REACH * width, (REACH + planes) * width)


def stencil(edges, cells, cells_b, cells_a, log_ext, slope, modes):
    modes_count, planes, width, lanes = modes.shape
    count = cells.shape[0]
    group = 4
    n_ext = planes + 2 * REACH + 2
    stride = (planes + 2 * REACH) * width + 8
    smem = pl.BlockSpec(memory_space=pltpu.SMEM)
    vmem = pl.BlockSpec(memory_space=pltpu.VMEM)
    shape = jax.ShapeDtypeStruct((modes_count, count), jnp.float32)
    return pl.pallas_call(
        functools.partial(stencil_kernel, planes, width, modes_count, group),
        grid=(modes_count // group,),
        out_shape=(shape, shape, shape),
        in_specs=[smem] * 4
        + [vmem, vmem, pl.BlockSpec((group, planes, width, lanes), lambda s: (s, 0, 0, 0))],
        out_specs=(pl.BlockSpec((modes_count, count), lambda s: (0, 0)),) * 3,
        scratch_shapes=[
            pltpu.VMEM((planes + 2 * REACH, 6, width, lanes), jnp.float32),
            pltpu.VMEM((planes, width, lanes), jnp.float32),
            pltpu.VMEM((n_ext * width + 16, lanes), jnp.float32),
            pltpu.VMEM((group, planes * width + 16, lanes), jnp.float32),
            pltpu.VMEM((group, (planes + 2) * width + 16, lanes), jnp.float32),
            pltpu.VMEM((modes_count * stride, lanes), jnp.float32),
        ],
        compiler_params=pltpu.CompilerParams(
            dimension_semantics=("arbitrary",), vmem_limit_bytes=40 * MIB
        ),
        cost_estimate=pl.CostEstimate(
            flops=40 * modes.size, bytes_accessed=4 * modes.size, transcendentals=0
        ),
        name="stencil",
    )(edges, cells, cells_b, cells_a, log_ext, slope, modes)


def solve_kernel(gram_ref, rhs_ref, out_ref, work):
    n = gram_ref.shape[0]
    f = rhs_ref.shape[1]
    work[...] = jnp.zeros_like(work)
    rows = lax.broadcasted_iota(jnp.int32, (n, n), 0)
    cols = lax.broadcasted_iota(jnp.int32, (n, n), 1)
    work[:, :n] = gram_ref[...] + jnp.where(rows == cols, 1.0, 0.0)
    work[:, n : n + f] = rhs_ref[...]
    matrix = work[...]
    tall = lax.broadcasted_iota(jnp.int32, matrix.shape, 0)
    for j in range(n):
        row = matrix[j : j + 1, :]
        row = row / row[:, j : j + 1]
        column = matrix[:, j : j + 1]
        matrix = jnp.where(tall == j, row, matrix - column * row)
    work[...] = matrix
    out_ref[...] = work[:, n : n + f]


def solve(gram, rhs):
    n, f = rhs.shape
    return pl.pallas_call(
        solve_kernel,
        out_shape=jax.ShapeDtypeStruct((n, f), jnp.float32),
        scratch_shapes=[pltpu.VMEM((n, 128 * pl.cdiv(n + f, 128)), jnp.float32)],
        name="solve",
    )(gram, rhs)


def update_kernel(place_ref, coef_ref, own_ref, others_ref, base_ref, out_ref, big):
    fields, deep, rows, lanes = out_ref.shape
    total = coef_ref.shape[0]
    mine = own_ref.shape[0]

    @pl.when(jnp.logical_and(pl.program_id(0) == 0, pl.program_id(1) == 0))
    def _():
        coef = coef_ref[...]
        high = coef.astype(jnp.bfloat16)
        low = (coef - high.astype(jnp.float32)).astype(jnp.bfloat16)
        tall, wide = fields * rows, total * rows
        r0 = lax.broadcasted_iota(jnp.int32, (tall, fields), 0)
        f0 = lax.broadcasted_iota(jnp.int32, (tall, fields), 1)
        spread_f = jnp.where(r0 // rows == f0, 1.0, 0.0).astype(jnp.bfloat16)
        k0 = lax.broadcasted_iota(jnp.int32, (total, wide), 0)
        c0 = lax.broadcasted_iota(jnp.int32, (total, wide), 1)
        spread_k = jnp.where(c0 // rows == k0, 1.0, 0.0).astype(jnp.bfloat16)
        r1 = lax.broadcasted_iota(jnp.int32, (tall, wide), 0)
        c1 = lax.broadcasted_iota(jnp.int32, (tall, wide), 1)
        same = r1 % rows == c1 % rows
        for p, part in enumerate((high, low)):
            a = lax.dot_general(
                spread_f, part, (((1,), (1,)), ((), ())), preferred_element_type=jnp.float32
            ).astype(jnp.bfloat16)
            b = jnp.dot(a, spread_k, preferred_element_type=jnp.float32)
            big[p * tall : (p + 1) * tall, :] = jnp.where(same, b, 0.0).astype(jnp.bfloat16)

    tall = fields * rows
    left = mine * rows

    def side(ref):
        count = ref.shape[0]
        return jnp.concatenate(
            [ref[:, d].reshape(count * rows, lanes) for d in range(deep)], axis=1
        )

    both = jnp.dot(big[:, :left], side(own_ref), preferred_element_type=jnp.float32)
    both = both + jnp.dot(big[:, left:], side(others_ref), preferred_element_type=jnp.float32)
    both = both[:tall] + both[tall:]
    for d in range(deep):
        part = both[:, d * lanes : (d + 1) * lanes].reshape(fields, rows, lanes)
        out_ref[:, d] = base_ref[:, d].astype(jnp.float32) + part


def update(place, coef, modes, others, base):
    fields, planes, width, lanes = base.shape
    mine = modes.shape[0]
    rest = others.shape[0]
    rows = 16
    deep = 2
    steps = width // rows

    def fixed(count):
        return pl.BlockSpec((count, deep, rows, lanes), lambda z, x, place: (0, z, x, 0))

    return pl.pallas_call(
        update_kernel,
        grid_spec=pltpu.PrefetchScalarGridSpec(
            num_scalar_prefetch=1,
            grid=(planes // deep, steps),
            in_specs=[
                pl.BlockSpec(coef.shape, lambda z, x, place: (0, 0)),
                pl.BlockSpec(
                    (mine, deep, rows, lanes),
                    lambda z, x, place: (0, z, place[0] * steps + x, 0),
                ),
                fixed(rest),
                fixed(fields),
            ],
            out_specs=fixed(fields),
            scratch_shapes=[
                pltpu.VMEM((2 * fields * rows, (mine + rest) * rows), jnp.bfloat16)
            ],
        ),
        out_shape=jax.ShapeDtypeStruct(base.shape, jnp.float32),
        compiler_params=pltpu.CompilerParams(
            dimension_semantics=("arbitrary", "arbitrary"), vmem_limit_bytes=32 * MIB
        ),
        name="update",
    )(place, coef, modes, others, base)


def on_device(log_cond, head_slope, modes, obs_cells, obs_var, misfit, base_fields):
    planes, width, lanes = log_cond.shape
    n_mode = lax.axis_size("mode")
    n_slab = lax.axis_size("slab")
    me = lax.axis_index("mode")
    level = lax.axis_index("slab")
    part = width // n_mode

    received = []
    for d in range(1, n_mode):
        to = (me + d) % n_mode
        piece = lax.dynamic_slice_in_dim(modes, to * part, part, axis=2)
        received.append(
            lax.ppermute(piece, "mode", [(i, (i + d) % n_mode) for i in range(n_mode)])
        )
    others = received[0] if n_mode == 2 else jnp.concatenate(received, axis=0)

    up = [(i, i + 1) for i in range(n_slab - 1)]
    down = [(i + 1, i) for i in range(n_slab - 1)]
    halo = REACH + 1
    cells_f = obs_cells.astype(jnp.float32).reshape(-1, lanes)

    def message(planes_out):
        return jnp.concatenate([planes_out.reshape(-1, lanes), cells_f], axis=0)

    from_below = lax.ppermute(message(log_cond[-halo:]), "slab", up)
    from_above = lax.ppermute(message(log_cond[:halo]), "slab", down)
    log_ext = jnp.concatenate(
        [
            from_below[: halo * width].reshape(halo, width, lanes),
            log_cond,
            from_above[: halo * width].reshape(halo, width, lanes),
        ],
        axis=0,
    )
    cells_b = from_below[halo * width :].reshape(-1).astype(jnp.int32)
    cells_a = from_above[halo * width :].reshape(-1).astype(jnp.int32)
    edges = jnp.stack([level == 0, level == n_slab - 1]).astype(jnp.int32)
    own, below, above = stencil(edges, obs_cells, cells_b, cells_a, log_ext, head_slope, modes)
    picked = own + lax.ppermute(above, "slab", up) + lax.ppermute(below, "slab", down)
    return picked, others, me


def finish(own, others, me, modes, obs_var, misfit, base_fields):
    n_mode = lax.axis_size("mode")
    mine = modes.shape[0]
    split = own.shape[1] // n_mode
    whole = lax.all_to_all(own, "mode", split_axis=1, concat_axis=0, tiled=True)
    var = lax.dynamic_slice_in_dim(obs_var, me * split, split, axis=0)
    miss = lax.dynamic_slice_in_dim(misfit, me * split, split, axis=0)
    scaled = whole / var[None, :]
    right = jnp.concatenate([whole.T, miss], axis=1)
    both = jnp.dot(scaled, right, precision=lax.Precision.HIGHEST)
    both = lax.psum(both, ("mode", "slab"))
    total = mine * n_mode
    coef = solve(both[:, :total], both[:, total:])
    order = (me - jnp.arange(n_mode)) % n_mode
    coef = coef.reshape(n_mode, mine, -1)[order].reshape(total, -1)
    return update(me.astype(jnp.int32).reshape(1), coef, modes, others, base_fields)


def both_phases(log_cond, head_slope, modes, obs_cells, obs_var, misfit, base_fields):
    picked, others, me = on_device(
        log_cond, head_slope, modes, obs_cells, obs_var, misfit, base_fields
    )
    return finish(picked, others, me, modes, obs_var, misfit, base_fields)


def solution(mesh):
    placed = (
        P("slab", None, None),
        P("slab", None, None),
        P("mode", "slab", None, None),
        P("slab"),
        P("slab"),
        P("slab", None),
        P(None, "slab", "mode", None),
    )
    return jax.shard_map(
        both_phases,
        mesh=mesh,
        in_specs=placed,
        out_specs=P(None, "slab", "mode", None),
        check_vma=False,
    )
```

```python
import functools
import math

import jax
import jax.numpy as jnp
from jax import lax
from jax.experimental import pallas as pl
from jax.experimental.pallas import tpu as pltpu
from jax.sharding import PartitionSpec as P

ITERS = 3
STORAGE = 0.05
REACH = ITERS - 1
MIB = 1 << 20


def sweep_weights(count):
    order = []
    low, high = (0, count - 1)
    while low <= high:
        order.append(low)
        if high != low:
            order.append(high)
        low += 1
        high -= 1
    return [1.0 / (1.15 + 0.85 * math.cos((2 * i + 1) * math.pi / (2 * count))) for i in order]


W0, W1, W2 = sweep_weights(ITERS)
SCALE_B = W0 * W1
SCALE_A = (1.0 - W1) * W0 + W1
SELF_2 = SCALE_A / SCALE_B
SELF_3 = (1.0 - W2) / W2
SOURCE_3 = 1.0 / SCALE_B


def stencil_kernel(
    planes, width, modes_count, group, edge_ref, cells_ref, cells_b_ref, cells_a_ref,
    log_ref, slope_ref, modes_ref, own_ref, below_ref, above_ref,
    coef, gain, cond, t_ref, u_ref, r_ref,
):
    step = pl.program_id(0)
    lanes = log_ref.shape[-1]
    pad = 8
    tiles = width // 8
    stride = (planes + 2 * REACH) * width + pad
    n_ext = planes + 2 * REACH + 2

    @pl.when(step == 0)
    def _():
        cond[...] = jnp.ones_like(cond)
        for z in range(n_ext):
            cond[pl.ds(pad + z * width, width), :] = jnp.exp(log_ref[z])

        @pl.when(edge_ref[0] == 1)
        def _():
            cond[pl.ds(pad + 2 * width, width), :] = cond[pl.ds(pad + 3 * width, width), :]

        @pl.when(edge_ref[1] == 1)
        def _():
            cond[pl.ds(pad + (planes + 3) * width, width), :] = cond[
                pl.ds(pad + (planes + 2) * width, width), :
            ]

        t_ref[...] = jnp.zeros_like(t_ref)
        u_ref[...] = jnp.zeros_like(u_ref)
        rows = lax.broadcasted_iota(jnp.int32, (8, lanes), 0)
        cols = lax.broadcasted_iota(jnp.int32, (8, lanes), 1)
        first = edge_ref[0] == 1
        last = edge_ref[1] == 1
        for z in range(planes + 2 * REACH):
            def body(i, carry, z=z):
                at = pad + (z + 1) * width + i * 8
                c = cond[pl.ds(at, 8), :]

                def harmonic(other):
                    return 2.0 * c * other / (c + other)

                x = rows + i * 8
                lower = harmonic(cond[pl.ds(at - width, 8), :])
                upper = harmonic(cond[pl.ds(at + width, 8), :])
                west = harmonic(jnp.where(x == 0, c, cond[pl.ds(at - 1, 8), :]))
                east = harmonic(jnp.where(x == width - 1, c, cond[pl.ds(at + 1, 8), :]))
                south = harmonic(jnp.where(cols == 0, c, pltpu.roll(c, 1, axis=1)))
                north = harmonic(jnp.where(cols == lanes - 1, c, pltpu.roll(c, lanes - 1, axis=1)))
                inverse = 1.0 / (STORAGE + lower + upper + west + east + south + north)
                zero = jnp.zeros_like(c)
                if z < REACH:
                    upper = jnp.where(first, zero, upper)
                if z == REACH:
                    lower = jnp.where(first, zero, lower)
                if z == REACH + planes - 1:
                    upper = jnp.where(last, zero, upper)
                if z >= REACH + planes:
                    lower = jnp.where(last, zero, lower)
                here = pl.ds(i * 8, 8)
                coef[z, 0, here, :] = lower * inverse
                coef[z, 1, here, :] = upper * inverse
                coef[z, 2, here, :] = jnp.where(x == 0, zero, west * inverse)
                coef[z, 3, here, :] = jnp.where(x == width - 1, zero, east * inverse)
                coef[z, 4, here, :] = jnp.where(cols == 0, zero, south * inverse)
                coef[z, 5, here, :] = jnp.where(cols == lanes - 1, zero, north * inverse)
                if REACH <= z < REACH + planes:
                    gain[z - REACH, here, :] = (
                        (W2 * SCALE_B) * slope_ref[z - REACH, here, :] * c * inverse
                    )
                return carry

            lax.fori_loop(0, tiles, body, 0, unroll=4)
        for k in range(modes_count):
            r_ref[pl.ds(k * stride + stride - pad, pad), :] = jnp.zeros((pad, lanes), jnp.float32)

    for z in range(planes):
        def convert(i, carry, z=z):
            here = pl.ds(i * 16, 16)
            g = gain[z, here, :]
            for m in range(group):
                t_ref[m, pl.ds(pad + z * width + i * 16, 16), :] = g * modes_ref[
                    m, z, here, :
                ].astype(jnp.float32)
            return carry

        lax.fori_loop(0, width // 16, convert, 0, unroll=4)

    def beside(ref, m, at, c, terms):
        total = None
        centre = ref[m, pl.ds(at, 8), :]
        for name in terms:
            if name == 0:
                v = ref[m, pl.ds(at - width, 8), :]
            elif name == 1:
                v = ref[m, pl.ds(at + width, 8), :]
            elif name == 2:
                v = ref[m, pl.ds(at - 1, 8), :]
            elif name == 3:
                v = ref[m, pl.ds(at + 1, 8), :]
            elif name == 4:
                v = pltpu.roll(centre, 1, axis=1)
            else:
                v = pltpu.roll(centre, lanes - 1, axis=1)
            v = c[name] * v
            total = v if total is None else total + v
        return centre, total

    for z in range(-1, planes + 1):
        if z == -1:
            terms = (1,)
        elif z == planes:
            terms = (0,)
        else:
            terms = (2, 3, 4, 5) + ((0,) if z > 0 else ()) + ((1,) if z < planes - 1 else ())

        def second(i, carry, z=z, terms=terms):
            c = {n: coef[z + REACH, n, pl.ds(i * 8, 8), :] for n in terms}
            at = pad + z * width + i * 8
            put = pl.ds(pad + (z + 1) * width + i * 8, 8)
            for m in range(group):
                if 0 <= z < planes:
                    centre, total = beside(t_ref, m, at, c, terms)
                    total = total + SELF_2 * centre
                elif z == -1:
                    total = c[1] * t_ref[m, pl.ds(at + width, 8), :]
                else:
                    total = c[0] * t_ref[m, pl.ds(at - width, 8), :]
                u_ref[m, put, :] = total
            return carry

        lax.fori_loop(0, tiles, second, 0, unroll=8)

    for z in range(-2, planes + 2):
        if z == -2:
            terms = (1,)
        elif z == planes + 1:
            terms = (0,)
        else:
            terms = (2, 3, 4, 5) + ((0,) if z > -1 else ()) + ((1,) if z < planes else ())

        def third(i, carry, z=z, terms=terms):
            c = {n: coef[z + REACH, n, pl.ds(i * 8, 8), :] for n in terms}
            at = pad + (z + 1) * width + i * 8
            for m in range(group):
                if z == -2:
                    total = c[1] * u_ref[m, pl.ds(at + width, 8), :]
                elif z == planes + 1:
                    total = c[0] * u_ref[m, pl.ds(at - width, 8), :]
                else:
                    centre, total = beside(u_ref, m, at, c, terms)
                    total = total + SELF_3 * centre
                    if 0 <= z < planes:
                        total = total + SOURCE_3 * t_ref[m, pl.ds(pad + z * width + i * 8, 8), :]
                put = pl.multiple_of(
                    (step * group + m) * stride + (z + REACH) * width + i * 8, 8
                )
                r_ref[pl.ds(put, 8), :] = total
            return carry

        lax.fori_loop(0, tiles, third, 0, unroll=8)

    @pl.when(step == pl.num_programs(0) - 1)
    def _():
        cols = lax.broadcasted_iota(jnp.int32, (modes_count, lanes), 1)
        count = cells_ref.shape[0]
        zero_row = stride - pad
        shift = lanes.bit_length() - 1

        def pick(cells, out, low, high, offset):
            def block(b, carry):
                def one(i, acc):
                    cell = cells[b * lanes + i]
                    row = cell >> shift
                    lane = cell & (lanes - 1)
                    if low is not None:
                        inside = jnp.logical_and(row >= low, row < high)
                        row = jnp.where(inside, row + offset, zero_row)
                    else:
                        row = row + offset
                    v = r_ref[pl.ds(row, modes_count, stride=stride), :]
                    v = pltpu.roll(v, (i - lane) & (lanes - 1), axis=1)
                    return jnp.where(cols == i, v, acc)

                acc = lax.fori_loop(
                    0, lanes, one, jnp.zeros((modes_count, lanes), jnp.float32), unroll=32
                )
                out[:, pl.ds(pl.multiple_of(b * lanes, lanes), lanes)] = acc
                return carry

            lax.fori_loop(0, count // lanes, block, 0)

        pick(cells_ref, own_ref, None, None, REACH * width)
        pick(
            cells_b_ref, below_ref, (planes - REACH) * width, planes * width,
            (REACH - planes) * width,
        )
        pick(cells_a_ref, above_ref, 0, REACH * width, (REACH + planes) * width)


def stencil(edges, cells, cells_b, cells_a, log_ext, slope, modes):
    modes_count, planes, width, lanes = modes.shape
    count = cells.shape[0]
    group = min(8, modes_count)
    n_ext = planes + 2 * REACH + 2
    stride = (planes + 2 * REACH) * width + 8
    smem = pl.BlockSpec(memory_space=pltpu.SMEM)
    vmem = pl.BlockSpec(memory_space=pltpu.VMEM)
    shape = jax.ShapeDtypeStruct((modes_count, count), jnp.float32)
    return pl.pallas_call(
        functools.partial(stencil_kernel, planes, width, modes_count, group),
        grid=(modes_count // group,),
        out_shape=(shape, shape, shape),
        in_specs=[smem] * 4
        + [vmem, vmem, pl.BlockSpec((group, planes, width, lanes), lambda s: (s, 0, 0, 0))],
        out_specs=(pl.BlockSpec((modes_count, count), lambda s: (0, 0)),) * 3,
        scratch_shapes=[
            pltpu.VMEM((planes + 2 * REACH, 6, width, lanes), jnp.float32),
            pltpu.VMEM((planes, width, lanes), jnp.float32),
            pltpu.VMEM((n_ext * width + 16, lanes), jnp.float32),
            pltpu.VMEM((group, planes * width + 16, lanes), jnp.float32),
            pltpu.VMEM((group, (planes + 2) * width + 16, lanes), jnp.float32),
            pltpu.VMEM((modes_count * stride, lanes), jnp.float32),
        ],
        compiler_params=pltpu.CompilerParams(
            dimension_semantics=("arbitrary",), vmem_limit_bytes=40 * MIB
        ),
        cost_estimate=pl.CostEstimate(
            flops=40 * modes.size, bytes_accessed=4 * modes.size, transcendentals=0
        ),
        name="stencil",
    )(edges, cells, cells_b, cells_a, log_ext, slope, modes)


def eliminate(matrix, n, block=4):
    tall = lax.broadcasted_iota(jnp.int32, matrix.shape, 0)
    for start in range(0, n, block):
        columns = [
            jnp.broadcast_to(matrix[:, j : j + 1], matrix.shape)
            for j in range(start, start + block)
        ]
        for i in range(block):
            j = start + i
            inverse = 1.0 / columns[i][j : j + 1, :]
            at = tall == j
            row = matrix[j : j + 1, :] * inverse
            matrix = jnp.where(at, row, matrix - columns[i] * row)
            for k in range(i + 1, block):
                entry = columns[k][j : j + 1, :] * inverse
                columns[k] = jnp.where(at, entry, columns[k] - columns[i] * entry)
    return matrix


def stages_of(n_mode, n_slab):
    stages = []
    stride = 1
    while stride < n_slab:
        radix = next(r for r in (4, 2, 3, n_slab // stride) if (n_slab // stride) % r == 0)
        stages.append((n_mode if stride == 1 else 1, stride, radix))
        stride *= radix
    return stages or [(n_mode, 1, 1)]


def reduce_kernel(
    n_mode, n_slab, stages, own, below, above, var, miss, out,
    in_b, in_a, picked, whole, sums, work,
    halo_send, halo_recv, mode_send, mode_recv, sum_send, sum_recv,
):
    me = lax.axis_index("mode")
    slab = lax.axis_index("slab")
    mine, count = own.shape
    split = count // n_mode
    n = mine * n_mode
    f = miss.shape[1]
    has_below = slab > 0
    has_above = slab < n_slab - 1
    slab_up = jnp.minimum(slab + 1, n_slab - 1)
    slab_down = jnp.maximum(slab - 1, 0)

    def member(stage, d):
        modes, stride, radix = stage
        low = lax.rem(slab // stride, radix)
        if modes == 1:
            return me, slab + (lax.rem(low + d, radix) - low) * stride
        g = lax.rem(me * radix + low + d, modes * radix)
        return g // radix, slab + (lax.rem(g, radix) - low) * stride

    @pl.when(jnp.logical_not(has_below))
    def _():
        in_b[...] = jnp.zeros_like(in_b)

    @pl.when(jnp.logical_not(has_above))
    def _():
        in_a[...] = jnp.zeros_like(in_a)

    barrier = pltpu.get_barrier_semaphore()

    def greet(device):
        pl.semaphore_signal(barrier, inc=1, device_id=device, device_id_type=pl.DeviceIdType.MESH)

    @pl.when(has_above)
    def _():
        greet((me, slab_up))

    @pl.when(has_below)
    def _():
        greet((me, slab_down))

    greeted = 0
    for d in range(1, n_mode):
        greet((lax.rem(me + d, n_mode), slab))
        greeted += 1
    for stage in stages:
        for d in range(1, stage[0] * stage[2]):
            greet(member(stage, d))
            greeted += 1
    ends = jnp.where(has_below, 1, 0) + jnp.where(has_above, 1, 0)
    pl.semaphore_wait(barrier, greeted + ends)

    def remote(src, dst, send, recv, device):
        return pltpu.make_async_remote_copy(
            src_ref=src, dst_ref=dst, send_sem=send, recv_sem=recv,
            device_id=device, device_id_type=pl.DeviceIdType.MESH,
        )

    going_up = remote(above, in_b, halo_send.at[0], halo_recv.at[0], (me, slab_up))
    going_down = remote(below, in_a, halo_send.at[1], halo_recv.at[1], (me, slab_down))

    @pl.when(has_above)
    def _():
        going_up.start()

    @pl.when(has_below)
    def _():
        going_down.start()

    @pl.when(has_below)
    def _():
        going_up.wait_recv()

    @pl.when(has_above)
    def _():
        going_down.wait_recv()

    picked[...] = own[...] + in_b[...] + in_a[...]

    copies = []
    for d in range(1, n_mode):
        to = lax.rem(me + d, n_mode)
        piece = pl.ds(pl.multiple_of(to * split, 128), split)
        copies.append(
            remote(picked.at[:, piece], whole.at[me], mode_send.at[d], mode_recv.at[d], (to, slab))
        )
        copies[-1].start()
    here = pl.ds(pl.multiple_of(me * split, 128), split)
    whole[me] = picked[:, here]
    for copy in copies:
        copy.wait_recv()
    every = whole[...].reshape(n, split)
    scaled = every / var[:, here]
    gram = lax.dot_general(
        scaled, every, (((1,), (1,)), ((), ())), precision=lax.Precision.HIGHEST,
        preferred_element_type=jnp.float32,
    )
    rows = pl.ds(pl.multiple_of(me * split, 8), split)
    rhs = jnp.dot(
        scaled, miss[rows, :], precision=lax.Precision.HIGHEST, preferred_element_type=jnp.float32
    )
    work[...] = jnp.zeros_like(work)
    work[:, :n] = gram
    work[:, n : n + f] = rhs

    base = 0
    sem = 0
    for stage in stages:
        size = stage[0] * stage[2]
        sums[base] = work[...]
        moving = []
        for d in range(1, size):
            moving.append(
                remote(sums.at[base], sums.at[base + d], sum_send.at[sem], sum_recv.at[sem],
                       member(stage, d))
            )
            moving[-1].start()
            sem += 1
        low = lax.rem(slab // stage[1], stage[2])
        if stage[0] > 1:
            low = low + me * stage[2]
        for copy in moving:
            copy.wait_recv()
        total = None
        for q in range(size):
            term = sums[base + lax.rem(low - q + size, size)]
            total = term if total is None else total + term
        work[...] = total
        copies += moving
        base += size

    matrix = work[...]
    tall = lax.broadcasted_iota(jnp.int32, matrix.shape, 0)
    wide = lax.broadcasted_iota(jnp.int32, matrix.shape, 1)
    work[...] = eliminate(matrix + jnp.where(tall == wide, 1.0, 0.0), n)
    for d in range(n_mode):
        block = lax.rem(me - d + n_mode, n_mode)
        out[d * mine : (d + 1) * mine, :] = work[
            pl.ds(pl.multiple_of(block * mine, 8), mine), n : n + f
        ]

    @pl.when(has_above)
    def _():
        going_up.wait_send()

    @pl.when(has_below)
    def _():
        going_down.wait_send()

    for copy in copies:
        copy.wait_send()


def reduce_and_solve(own, below, above, obs_var, misfit):
    n_mode = lax.axis_size("mode")
    n_slab = lax.axis_size("slab")
    mine, count = own.shape
    n = mine * n_mode
    f = misfit.shape[1]
    stages = stages_of(n_mode, n_slab)
    slots = sum(s[0] * s[2] for s in stages)
    wide = 128 * pl.cdiv(n + f, 128)
    vmem = pl.BlockSpec(memory_space=pltpu.VMEM)
    dma = pltpu.SemaphoreType.DMA
    return pl.pallas_call(
        functools.partial(reduce_kernel, n_mode, n_slab, stages),
        out_shape=jax.ShapeDtypeStruct((n, f), jnp.float32),
        in_specs=[vmem] * 5,
        out_specs=vmem,
        scratch_shapes=[
            pltpu.VMEM((mine, count), jnp.float32),
            pltpu.VMEM((mine, count), jnp.float32),
            pltpu.VMEM((mine, count), jnp.float32),
            pltpu.VMEM((n_mode, mine, count // n_mode), jnp.float32),
            pltpu.VMEM((slots, n, wide), jnp.float32),
            pltpu.VMEM((n, wide), jnp.float32),
            dma((2,)), dma((2,)), dma((n_mode,)), dma((n_mode,)), dma((slots,)), dma((slots,)),
        ],
        compiler_params=pltpu.CompilerParams(
            collective_id=0, has_side_effects=True, vmem_limit_bytes=24 * MIB
        ),
        cost_estimate=pl.CostEstimate(
            flops=2 * n * n * count, bytes_accessed=1 << 20, transcendentals=0
        ),
        name="reduce_and_solve",
    )(own, below, above, obs_var.reshape(1, count), misfit)


def update_kernel(place_ref, coef_ref, own_ref, others_ref, base_ref, out_ref, big):
    fields, deep, rows, lanes = out_ref.shape
    total = coef_ref.shape[0]
    mine = own_ref.shape[0]

    @pl.when(jnp.logical_and(pl.program_id(0) == 0, pl.program_id(1) == 0))
    def _():
        coef = coef_ref[...]
        high = coef.astype(jnp.bfloat16)
        low = (coef - high.astype(jnp.float32)).astype(jnp.bfloat16)
        tall, wide = fields * rows, total * rows
        r0 = lax.broadcasted_iota(jnp.int32, (tall, fields), 0)
        f0 = lax.broadcasted_iota(jnp.int32, (tall, fields), 1)
        spread_f = jnp.where(r0 // rows == f0, 1.0, 0.0).astype(jnp.bfloat16)
        k0 = lax.broadcasted_iota(jnp.int32, (total, wide), 0)
        c0 = lax.broadcasted_iota(jnp.int32, (total, wide), 1)
        spread_k = jnp.where(c0 // rows == k0, 1.0, 0.0).astype(jnp.bfloat16)
        r1 = lax.broadcasted_iota(jnp.int32, (tall, wide), 0)
        c1 = lax.broadcasted_iota(jnp.int32, (tall, wide), 1)
        same = r1 % rows == c1 % rows
        for p, part in enumerate((high, low)):
            a = lax.dot_general(
                spread_f, part, (((1,), (1,)), ((), ())), preferred_element_type=jnp.float32
            ).astype(jnp.bfloat16)
            b = jnp.dot(a, spread_k, preferred_element_type=jnp.float32)
            big[p * tall : (p + 1) * tall, :] = jnp.where(same, b, 0.0).astype(jnp.bfloat16)

    tall = fields * rows
    left = mine * rows

    def side(ref):
        count = ref.shape[0]
        return jnp.concatenate(
            [ref[:, d].reshape(count * rows, lanes) for d in range(deep)], axis=1
        )

    both = jnp.dot(big[:, :left], side(own_ref), preferred_element_type=jnp.float32)
    both = both + jnp.dot(big[:, left:], side(others_ref), preferred_element_type=jnp.float32)
    both = both[:tall] + both[tall:]
    for d in range(deep):
        part = both[:, d * lanes : (d + 1) * lanes].reshape(fields, rows, lanes)
        out_ref[:, d] = base_ref[:, d].astype(jnp.float32) + part


def update(place, coef, modes, others, base):
    fields, planes, width, lanes = base.shape
    mine = modes.shape[0]
    rest = others.shape[0]
    rows = 16
    deep = 2
    steps = width // rows

    def fixed(count):
        return pl.BlockSpec((count, deep, rows, lanes), lambda z, x, place: (0, z, x, 0))

    return pl.pallas_call(
        update_kernel,
        grid_spec=pltpu.PrefetchScalarGridSpec(
            num_scalar_prefetch=1,
            grid=(planes // deep, steps),
            in_specs=[
                pl.BlockSpec(coef.shape, lambda z, x, place: (0, 0)),
                pl.BlockSpec(
                    (mine, deep, rows, lanes),
                    lambda z, x, place: (0, z, place[0] * steps + x, 0),
                ),
                fixed(rest),
                fixed(fields),
            ],
            out_specs=fixed(fields),
            scratch_shapes=[
                pltpu.VMEM((2 * fields * rows, (mine + rest) * rows), jnp.bfloat16)
            ],
        ),
        out_shape=jax.ShapeDtypeStruct(base.shape, jnp.float32),
        compiler_params=pltpu.CompilerParams(
            dimension_semantics=("arbitrary", "arbitrary"), vmem_limit_bytes=32 * MIB
        ),
        name="update",
    )(place, coef, modes, others, base)


def on_device(log_cond, head_slope, modes, obs_cells, obs_var, misfit, base_fields):
    planes, width, lanes = log_cond.shape
    n_mode = lax.axis_size("mode")
    n_slab = lax.axis_size("slab")
    me = lax.axis_index("mode")
    level = lax.axis_index("slab")
    part = width // n_mode

    received = []
    for d in range(1, n_mode):
        to = (me + d) % n_mode
        piece = lax.dynamic_slice_in_dim(modes, to * part, part, axis=2)
        received.append(
            lax.ppermute(piece, "mode", [(i, (i + d) % n_mode) for i in range(n_mode)])
        )
    others = received[0] if n_mode == 2 else jnp.concatenate(received, axis=0)

    up = [(i, i + 1) for i in range(n_slab - 1)]
    down = [(i + 1, i) for i in range(n_slab - 1)]
    halo = REACH + 1
    cells_f = obs_cells.astype(jnp.float32).reshape(-1, lanes)

    def message(planes_out):
        return jnp.concatenate([planes_out.reshape(-1, lanes), cells_f], axis=0)

    from_below = lax.ppermute(message(log_cond[-halo:]), "slab", up)
    from_above = lax.ppermute(message(log_cond[:halo]), "slab", down)
    log_ext = jnp.concatenate(
        [
            from_below[: halo * width].reshape(halo, width, lanes),
            log_cond,
            from_above[: halo * width].reshape(halo, width, lanes),
        ],
        axis=0,
    )
    cells_b = from_below[halo * width :].reshape(-1).astype(jnp.int32)
    cells_a = from_above[halo * width :].reshape(-1).astype(jnp.int32)
    edges = jnp.stack([level == 0, level == n_slab - 1]).astype(jnp.int32)
    own, below, above = stencil(edges, obs_cells, cells_b, cells_a, log_ext, head_slope, modes)
    coef = reduce_and_solve(own, below, above, obs_var, misfit)
    return update(me.astype(jnp.int32).reshape(1), coef, modes, others, base_fields)


def solution(mesh):
    placed = (
        P("slab", None, None),
        P("slab", None, None),
        P("mode", "slab", None, None),
        P("slab"),
        P("slab"),
        P("slab", None),
        P(None, "slab", "mode", None),
    )
    return jax.shard_map(
        on_device,
        mesh=mesh,
        in_specs=placed,
        out_specs=P(None, "slab", "mode", None),
        check_vma=False,
    )
```

```python
import functools
import math

import jax
import jax.numpy as jnp
from jax import lax
from jax.experimental import pallas as pl
from jax.experimental.pallas import tpu as pltpu
from jax.sharding import PartitionSpec as P

ITERS = 3
STORAGE = 0.05
REACH = ITERS - 1
MIB = 1 << 20
ROWS = 8


def sweep_weights(count):
    order = []
    low, high = (0, count - 1)
    while low <= high:
        order.append(low)
        if high != low:
            order.append(high)
        low += 1
        high -= 1
    return [1.0 / (1.15 + 0.85 * math.cos((2 * i + 1) * math.pi / (2 * count))) for i in order]


W0, W1, W2 = sweep_weights(ITERS)
SCALE_B = W0 * W1
SCALE_A = (1.0 - W1) * W0 + W1
SELF_2 = SCALE_A / SCALE_B
SELF_3 = (1.0 - W2) / W2
SOURCE_3 = 1.0 / SCALE_B


def stencil_kernel(
    planes, width, modes_count, group, edge_ref, cells_ref, cells_b_ref, cells_a_ref,
    log_ref, slope_ref, modes_ref, own_ref, below_ref, above_ref,
    coef, gain, cond, t_ref, u_ref, r_ref,
):
    step = pl.program_id(0)
    lanes = log_ref.shape[-1]
    pad = 8
    tiles = width // 8
    stride = (planes + 2 * REACH) * width + pad
    n_ext = planes + 2 * REACH + 2

    @pl.when(step == 0)
    def _():
        cond[...] = jnp.ones_like(cond)
        for z in range(n_ext):
            cond[pl.ds(pad + z * width, width), :] = jnp.exp(log_ref[z])

        @pl.when(edge_ref[0] == 1)
        def _():
            cond[pl.ds(pad + 2 * width, width), :] = cond[pl.ds(pad + 3 * width, width), :]

        @pl.when(edge_ref[1] == 1)
        def _():
            cond[pl.ds(pad + (planes + 3) * width, width), :] = cond[
                pl.ds(pad + (planes + 2) * width, width), :
            ]

        t_ref[...] = jnp.zeros_like(t_ref)
        u_ref[...] = jnp.zeros_like(u_ref)
        rows = lax.broadcasted_iota(jnp.int32, (8, lanes), 0)
        cols = lax.broadcasted_iota(jnp.int32, (8, lanes), 1)
        first = edge_ref[0] == 1
        last = edge_ref[1] == 1
        for z in range(planes + 2 * REACH):
            def body(i, carry, z=z):
                at = pad + (z + 1) * width + i * 8
                c = cond[pl.ds(at, 8), :]

                def harmonic(other):
                    return 2.0 * c * other / (c + other)

                x = rows + i * 8
                lower = harmonic(cond[pl.ds(at - width, 8), :])
                upper = harmonic(cond[pl.ds(at + width, 8), :])
                west = harmonic(jnp.where(x == 0, c, cond[pl.ds(at - 1, 8), :]))
                east = harmonic(jnp.where(x == width - 1, c, cond[pl.ds(at + 1, 8), :]))
                south = harmonic(jnp.where(cols == 0, c, pltpu.roll(c, 1, axis=1)))
                north = harmonic(jnp.where(cols == lanes - 1, c, pltpu.roll(c, lanes - 1, axis=1)))
                inverse = 1.0 / (STORAGE + lower + upper + west + east + south + north)
                zero = jnp.zeros_like(c)
                if z < REACH:
                    upper = jnp.where(first, zero, upper)
                if z == REACH:
                    lower = jnp.where(first, zero, lower)
                if z == REACH + planes - 1:
                    upper = jnp.where(last, zero, upper)
                if z >= REACH + planes:
                    lower = jnp.where(last, zero, lower)
                here = pl.ds(i * 8, 8)
                coef[z, 0, here, :] = lower * inverse
                coef[z, 1, here, :] = upper * inverse
                coef[z, 2, here, :] = jnp.where(x == 0, zero, west * inverse)
                coef[z, 3, here, :] = jnp.where(x == width - 1, zero, east * inverse)
                coef[z, 4, here, :] = jnp.where(cols == 0, zero, south * inverse)
                coef[z, 5, here, :] = jnp.where(cols == lanes - 1, zero, north * inverse)
                if REACH <= z < REACH + planes:
                    gain[z - REACH, here, :] = (
                        (W2 * SCALE_B) * slope_ref[z - REACH, here, :] * c * inverse
                    )
                return carry

            lax.fori_loop(0, tiles, body, 0, unroll=8)
        for k in range(modes_count):
            r_ref[pl.ds(k * stride + stride - pad, pad), :] = jnp.zeros((pad, lanes), jnp.float32)

    for z in range(planes):
        def convert(i, carry, z=z):
            here = pl.ds(i * 16, 16)
            g = gain[z, here, :]
            for m in range(group):
                t_ref[m, pl.ds(pad + z * width + i * 16, 16), :] = g * modes_ref[
                    m, z, here, :
                ].astype(jnp.float32)
            return carry

        lax.fori_loop(0, width // 16, convert, 0, unroll=8)

    def beside(ref, m, at, c, terms):
        total = None
        centre = ref[m, pl.ds(at, 8), :]
        for name in terms:
            if name == 0:
                v = ref[m, pl.ds(at - width, 8), :]
            elif name == 1:
                v = ref[m, pl.ds(at + width, 8), :]
            elif name == 2:
                v = ref[m, pl.ds(at - 1, 8), :]
            elif name == 3:
                v = ref[m, pl.ds(at + 1, 8), :]
            elif name == 4:
                v = pltpu.roll(centre, 1, axis=1)
            else:
                v = pltpu.roll(centre, lanes - 1, axis=1)
            v = c[name] * v
            total = v if total is None else total + v
        return centre, total

    for z in range(-1, planes + 1):
        if z == -1:
            terms = (1,)
        elif z == planes:
            terms = (0,)
        else:
            terms = (2, 3, 4, 5) + ((0,) if z > 0 else ()) + ((1,) if z < planes - 1 else ())

        def second(i, carry, z=z, terms=terms):
            c = {n: coef[z + REACH, n, pl.ds(i * 8, 8), :] for n in terms}
            at = pad + z * width + i * 8
            put = pl.ds(pad + (z + 1) * width + i * 8, 8)
            for m in range(group):
                if 0 <= z < planes:
                    centre, total = beside(t_ref, m, at, c, terms)
                    total = total + SELF_2 * centre
                elif z == -1:
                    total = c[1] * t_ref[m, pl.ds(at + width, 8), :]
                else:
                    total = c[0] * t_ref[m, pl.ds(at - width, 8), :]
                u_ref[m, put, :] = total
            return carry

        lax.fori_loop(0, tiles, second, 0, unroll=tiles)

    for z in range(-2, planes + 2):
        if z == -2:
            terms = (1,)
        elif z == planes + 1:
            terms = (0,)
        else:
            terms = (2, 3, 4, 5) + ((0,) if z > -1 else ()) + ((1,) if z < planes else ())

        def third(i, carry, z=z, terms=terms):
            c = {n: coef[z + REACH, n, pl.ds(i * 8, 8), :] for n in terms}
            at = pad + (z + 1) * width + i * 8
            for m in range(group):
                if z == -2:
                    total = c[1] * u_ref[m, pl.ds(at + width, 8), :]
                elif z == planes + 1:
                    total = c[0] * u_ref[m, pl.ds(at - width, 8), :]
                else:
                    centre, total = beside(u_ref, m, at, c, terms)
                    total = total + SELF_3 * centre
                    if 0 <= z < planes:
                        total = total + SOURCE_3 * t_ref[m, pl.ds(pad + z * width + i * 8, 8), :]
                put = pl.multiple_of(
                    (step * group + m) * stride + (z + REACH) * width + i * 8, 8
                )
                r_ref[pl.ds(put, 8), :] = total
            return carry

        lax.fori_loop(0, tiles, third, 0, unroll=tiles)

    @pl.when(step == pl.num_programs(0) - 1)
    def _():
        cols = lax.broadcasted_iota(jnp.int32, (modes_count, lanes), 1)
        count = cells_ref.shape[0]
        zero_row = stride - pad
        shift = lanes.bit_length() - 1

        def pick(cells, out, low, high, offset):
            def block(b, carry):
                def one(i, acc):
                    cell = cells[b * lanes + i]
                    row = cell >> shift
                    lane = cell & (lanes - 1)
                    if low is not None:
                        inside = jnp.logical_and(row >= low, row < high)
                        row = jnp.where(inside, row + offset, zero_row)
                    else:
                        row = row + offset
                    v = r_ref[pl.ds(row, modes_count, stride=stride), :]
                    v = pltpu.roll(v, (i - lane) & (lanes - 1), axis=1)
                    return jnp.where(cols == i, v, acc)

                acc = lax.fori_loop(
                    0, lanes, one, jnp.zeros((modes_count, lanes), jnp.float32), unroll=lanes
                )
                out[:, pl.ds(pl.multiple_of(b * lanes, lanes), lanes)] = acc
                return carry

            lax.fori_loop(0, count // lanes, block, 0)

        pick(cells_ref, own_ref, None, None, REACH * width)
        pick(
            cells_b_ref, below_ref, (planes - REACH) * width, planes * width,
            (REACH - planes) * width,
        )
        pick(cells_a_ref, above_ref, 0, REACH * width, (REACH + planes) * width)


def stencil(edges, cells, cells_b, cells_a, log_ext, slope, modes):
    modes_count, planes, width, lanes = modes.shape
    count = cells.shape[0]
    group = min(8, modes_count)
    n_ext = planes + 2 * REACH + 2
    stride = (planes + 2 * REACH) * width + 8
    smem = pl.BlockSpec(memory_space=pltpu.SMEM)
    vmem = pl.BlockSpec(memory_space=pltpu.VMEM)
    shape = jax.ShapeDtypeStruct((modes_count, count), jnp.float32)
    return pl.pallas_call(
        functools.partial(stencil_kernel, planes, width, modes_count, group),
        grid=(modes_count // group,),
        out_shape=(shape, shape, shape),
        in_specs=[smem] * 4
        + [vmem, vmem, pl.BlockSpec((group, planes, width, lanes), lambda s: (s, 0, 0, 0))],
        out_specs=(pl.BlockSpec((modes_count, count), lambda s: (0, 0)),) * 3,
        scratch_shapes=[
            pltpu.VMEM((planes + 2 * REACH, 6, width, lanes), jnp.float32),
            pltpu.VMEM((planes, width, lanes), jnp.float32),
            pltpu.VMEM((n_ext * width + 16, lanes), jnp.float32),
            pltpu.VMEM((group, planes * width + 16, lanes), jnp.float32),
            pltpu.VMEM((group, (planes + 2) * width + 16, lanes), jnp.float32),
            pltpu.VMEM((modes_count * stride, lanes), jnp.float32),
        ],
        compiler_params=pltpu.CompilerParams(
            dimension_semantics=("arbitrary",), vmem_limit_bytes=46 * MIB
        ),
        cost_estimate=pl.CostEstimate(
            flops=40 * modes.size, bytes_accessed=4 * modes.size, transcendentals=0
        ),
        name="stencil",
    )(edges, cells, cells_b, cells_a, log_ext, slope, modes)


def eliminate(matrix, n, block=4):
    tall = lax.broadcasted_iota(jnp.int32, matrix.shape, 0)
    for start in range(0, n, block):
        columns = [
            jnp.broadcast_to(matrix[:, j : j + 1], matrix.shape)
            for j in range(start, start + block)
        ]
        for i in range(block):
            j = start + i
            inverse = 1.0 / columns[i][j : j + 1, :]
            at = tall == j
            row = matrix[j : j + 1, :] * inverse
            matrix = jnp.where(at, row, matrix - columns[i] * row)
            for k in range(i + 1, block):
                entry = columns[k][j : j + 1, :] * inverse
                columns[k] = jnp.where(at, entry, columns[k] - columns[i] * entry)
    return matrix


def stages_of(n_mode, n_slab):
    stages = []
    stride = 1
    while stride < n_slab:
        radix = next(r for r in (4, 2, 3, n_slab // stride) if (n_slab // stride) % r == 0)
        stages.append((n_mode if stride == 1 else 1, stride, radix))
        stride *= radix
    return stages or [(n_mode, 1, 1)]


def reduce_kernel(
    n_mode, n_slab, stages, own, below, above, var, miss, out,
    in_b, in_a, picked, whole, sums, work,
    halo_send, halo_recv, mode_send, mode_recv, sum_send, sum_recv,
):
    me = lax.axis_index("mode")
    slab = lax.axis_index("slab")
    mine, count = own.shape
    split = count // n_mode
    n = mine * n_mode
    f = miss.shape[0]
    has_below = slab > 0
    has_above = slab < n_slab - 1
    slab_up = jnp.minimum(slab + 1, n_slab - 1)
    slab_down = jnp.maximum(slab - 1, 0)

    def member(stage, d):
        modes, stride, radix = stage
        low = lax.rem(slab // stride, radix)
        if modes == 1:
            return me, slab + (lax.rem(low + d, radix) - low) * stride
        g = lax.rem(me * radix + low + d, modes * radix)
        return g // radix, slab + (lax.rem(g, radix) - low) * stride

    @pl.when(jnp.logical_not(has_below))
    def _():
        in_b[...] = jnp.zeros_like(in_b)

    @pl.when(jnp.logical_not(has_above))
    def _():
        in_a[...] = jnp.zeros_like(in_a)

    barrier = pltpu.get_barrier_semaphore()

    def greet(device):
        pl.semaphore_signal(barrier, inc=1, device_id=device, device_id_type=pl.DeviceIdType.MESH)

    @pl.when(has_above)
    def _():
        greet((me, slab_up))

    @pl.when(has_below)
    def _():
        greet((me, slab_down))

    greeted = 0
    for d in range(1, n_mode):
        greet((lax.rem(me + d, n_mode), slab))
        greeted += 1
    for stage in stages:
        for d in range(1, stage[0] * stage[2]):
            greet(member(stage, d))
            greeted += 1
    ends = jnp.where(has_below, 1, 0) + jnp.where(has_above, 1, 0)
    pl.semaphore_wait(barrier, greeted + ends)

    def remote(src, dst, send, recv, device):
        return pltpu.make_async_remote_copy(
            src_ref=src, dst_ref=dst, send_sem=send, recv_sem=recv,
            device_id=device, device_id_type=pl.DeviceIdType.MESH,
        )

    going_up = remote(above, in_b, halo_send.at[0], halo_recv.at[0], (me, slab_up))
    going_down = remote(below, in_a, halo_send.at[1], halo_recv.at[1], (me, slab_down))

    @pl.when(has_above)
    def _():
        going_up.start()

    @pl.when(has_below)
    def _():
        going_down.start()

    @pl.when(has_below)
    def _():
        going_up.wait_recv()

    @pl.when(has_above)
    def _():
        going_down.wait_recv()

    picked[...] = own[...] + in_b[...] + in_a[...]

    copies = []
    for d in range(1, n_mode):
        to = lax.rem(me + d, n_mode)
        piece = pl.ds(pl.multiple_of(to * split, 128), split)
        copies.append(
            remote(picked.at[:, piece], whole.at[me], mode_send.at[d], mode_recv.at[d], (to, slab))
        )
        copies[-1].start()
    here = pl.ds(pl.multiple_of(me * split, 128), split)
    whole[me] = picked[:, here]
    for copy in copies:
        copy.wait_recv()
    every = whole[...].reshape(n, split)
    scaled = every / var[:, here]
    gram = lax.dot_general(
        scaled, every, (((1,), (1,)), ((), ())), precision=lax.Precision.HIGHEST,
        preferred_element_type=jnp.float32,
    )
    rhs = lax.dot_general(
        scaled, miss[:, here], (((1,), (1,)), ((), ())), precision=lax.Precision.HIGHEST,
        preferred_element_type=jnp.float32,
    )
    work[...] = jnp.zeros_like(work)
    work[:, :n] = gram
    work[:, n : n + f] = rhs

    base = 0
    sem = 0
    for stage in stages:
        size = stage[0] * stage[2]
        sums[base] = work[...]
        moving = []
        for d in range(1, size):
            moving.append(
                remote(sums.at[base], sums.at[base + d], sum_send.at[sem], sum_recv.at[sem],
                       member(stage, d))
            )
            moving[-1].start()
            sem += 1
        low = lax.rem(slab // stage[1], stage[2])
        if stage[0] > 1:
            low = low + me * stage[2]
        for copy in moving:
            copy.wait_recv()
        total = None
        for q in range(size):
            term = sums[base + lax.rem(low - q + size, size)]
            total = term if total is None else total + term
        work[...] = total
        copies += moving
        base += size

    matrix = work[...]
    tall = lax.broadcasted_iota(jnp.int32, matrix.shape, 0)
    wide = lax.broadcasted_iota(jnp.int32, matrix.shape, 1)
    work[...] = eliminate(matrix + jnp.where(tall == wide, 1.0, 0.0), n)
    for d in range(n_mode):
        block = lax.rem(me - d + n_mode, n_mode)
        out[d * mine : (d + 1) * mine, :] = work[
            pl.ds(pl.multiple_of(block * mine, 8), mine), n : n + f
        ]

    @pl.when(has_above)
    def _():
        going_up.wait_send()

    @pl.when(has_below)
    def _():
        going_down.wait_send()

    for copy in copies:
        copy.wait_send()


def reduce_and_solve(own, below, above, obs_var, misfit):
    n_mode = lax.axis_size("mode")
    n_slab = lax.axis_size("slab")
    mine, count = own.shape
    n = mine * n_mode
    f = misfit.shape[1]
    stages = stages_of(n_mode, n_slab)
    slots = sum(s[0] * s[2] for s in stages)
    wide = 128 * pl.cdiv(n + f, 128)
    vmem = pl.BlockSpec(memory_space=pltpu.VMEM)
    dma = pltpu.SemaphoreType.DMA
    return pl.pallas_call(
        functools.partial(reduce_kernel, n_mode, n_slab, stages),
        out_shape=jax.ShapeDtypeStruct((n, f), jnp.float32),
        in_specs=[vmem] * 5,
        out_specs=vmem,
        scratch_shapes=[
            pltpu.VMEM((mine, count), jnp.float32),
            pltpu.VMEM((mine, count), jnp.float32),
            pltpu.VMEM((mine, count), jnp.float32),
            pltpu.VMEM((n_mode, mine, count // n_mode), jnp.float32),
            pltpu.VMEM((slots, n, wide), jnp.float32),
            pltpu.VMEM((n, wide), jnp.float32),
            dma((2,)), dma((2,)), dma((n_mode,)), dma((n_mode,)), dma((slots,)), dma((slots,)),
        ],
        compiler_params=pltpu.CompilerParams(
            collective_id=0, has_side_effects=True, vmem_limit_bytes=24 * MIB
        ),
        cost_estimate=pl.CostEstimate(
            flops=2 * n * n * count, bytes_accessed=1 << 20, transcendentals=0
        ),
        name="reduce_and_solve",
    )(own, below, above, obs_var.reshape(1, count), misfit.T)


def update_kernel(place_ref, coef_ref, own_ref, others_ref, base_ref, out_ref, big):
    fields, deep, rows, lanes = out_ref.shape
    total = coef_ref.shape[0]
    mine = own_ref.shape[0]

    @pl.when(jnp.logical_and(pl.program_id(0) == 0, pl.program_id(1) == 0))
    def _():
        coef = coef_ref[...]
        high = coef.astype(jnp.bfloat16)
        low = (coef - high.astype(jnp.float32)).astype(jnp.bfloat16)
        tall, wide = fields * ROWS, total * ROWS
        r0 = lax.broadcasted_iota(jnp.int32, (tall, fields), 0)
        f0 = lax.broadcasted_iota(jnp.int32, (tall, fields), 1)
        spread_f = jnp.where(r0 // ROWS == f0, 1.0, 0.0).astype(jnp.bfloat16)
        k0 = lax.broadcasted_iota(jnp.int32, (total, wide), 0)
        c0 = lax.broadcasted_iota(jnp.int32, (total, wide), 1)
        spread_k = jnp.where(c0 // ROWS == k0, 1.0, 0.0).astype(jnp.bfloat16)
        r1 = lax.broadcasted_iota(jnp.int32, (tall, wide), 0)
        c1 = lax.broadcasted_iota(jnp.int32, (tall, wide), 1)
        same = r1 % ROWS == c1 % ROWS
        for p, part in enumerate((high, low)):
            a = lax.dot_general(
                spread_f, part, (((1,), (1,)), ((), ())), preferred_element_type=jnp.float32
            ).astype(jnp.bfloat16)
            b = jnp.dot(a, spread_k, preferred_element_type=jnp.float32)
            big[p * tall : (p + 1) * tall, :] = jnp.where(same, b, 0.0).astype(jnp.bfloat16)

    tall = fields * ROWS
    left = mine * ROWS

    def side(ref):
        count = ref.shape[0]
        tiles = []
        for d in range(deep):
            whole = ref[:, d].astype(jnp.float32)
            for h in range(rows // ROWS):
                tile = whole[:, h * ROWS : (h + 1) * ROWS, :]
                tiles.append(tile.reshape(count * ROWS, lanes).astype(jnp.bfloat16))
        return jnp.concatenate(tiles, axis=1)

    both = jnp.dot(big[:, :left], side(own_ref), preferred_element_type=jnp.float32)
    both = both + jnp.dot(big[:, left:], side(others_ref), preferred_element_type=jnp.float32)
    both = both[:tall] + both[tall:]
    for d in range(deep):
        base = base_ref[:, d].astype(jnp.float32)
        for h in range(rows // ROWS):
            at = (d * (rows // ROWS) + h) * lanes
            part = both[:, at : at + lanes].reshape(fields, ROWS, lanes)
            out_ref[:, d, h * ROWS : (h + 1) * ROWS, :] = (
                base[:, h * ROWS : (h + 1) * ROWS, :] + part
            )


def update(place, coef, modes, others, base):
    fields, planes, width, lanes = base.shape
    mine = modes.shape[0]
    rest = others.shape[0]
    rows = 16
    deep = 2
    steps = width // rows

    def fixed(count):
        return pl.BlockSpec((count, deep, rows, lanes), lambda z, x, place: (0, z, x, 0))

    return pl.pallas_call(
        update_kernel,
        grid_spec=pltpu.PrefetchScalarGridSpec(
            num_scalar_prefetch=1,
            grid=(planes // deep, steps),
            in_specs=[
                pl.BlockSpec(coef.shape, lambda z, x, place: (0, 0)),
                pl.BlockSpec(
                    (mine, deep, rows, lanes),
                    lambda z, x, place: (0, z, place[0] * steps + x, 0),
                ),
                fixed(rest),
                fixed(fields),
            ],
            out_specs=fixed(fields),
            scratch_shapes=[
                pltpu.VMEM((2 * fields * ROWS, (mine + rest) * ROWS), jnp.bfloat16)
            ],
        ),
        out_shape=jax.ShapeDtypeStruct(base.shape, jnp.float32),
        compiler_params=pltpu.CompilerParams(
            dimension_semantics=("arbitrary", "arbitrary"), vmem_limit_bytes=32 * MIB
        ),
        name="update",
    )(place, coef, modes, others, base)


def on_device(log_cond, head_slope, modes, obs_cells, obs_var, misfit, base_fields):
    planes, width, lanes = log_cond.shape
    n_mode = lax.axis_size("mode")
    n_slab = lax.axis_size("slab")
    me = lax.axis_index("mode")
    level = lax.axis_index("slab")
    part = width // n_mode

    up = [(i, i + 1) for i in range(n_slab - 1)]
    down = [(i + 1, i) for i in range(n_slab - 1)]
    halo = REACH + 1
    cells_f = obs_cells.astype(jnp.float32).reshape(-1, lanes)

    def message(planes_out):
        return jnp.concatenate([planes_out.reshape(-1, lanes), cells_f], axis=0)

    to_above, to_below, modes = lax.optimization_barrier(
        (message(log_cond[-halo:]), message(log_cond[:halo]), modes)
    )
    from_below = lax.ppermute(to_above, "slab", up)
    from_above = lax.ppermute(to_below, "slab", down)
    received = []
    for d in range(1, n_mode):
        to = (me + d) % n_mode
        piece = lax.dynamic_slice_in_dim(modes, to * part, part, axis=2)
        received.append(
            lax.ppermute(piece, "mode", [(i, (i + d) % n_mode) for i in range(n_mode)])
        )
    others = received[0] if n_mode == 2 else jnp.concatenate(received, axis=0)

    log_ext = jnp.concatenate(
        [
            from_below[: halo * width].reshape(halo, width, lanes),
            log_cond,
            from_above[: halo * width].reshape(halo, width, lanes),
        ],
        axis=0,
    )
    cells_b = from_below[halo * width :].reshape(-1).astype(jnp.int32)
    cells_a = from_above[halo * width :].reshape(-1).astype(jnp.int32)
    edges = jnp.stack([level == 0, level == n_slab - 1]).astype(jnp.int32)
    own, below, above = stencil(edges, obs_cells, cells_b, cells_a, log_ext, head_slope, modes)
    coef = reduce_and_solve(own, below, above, obs_var, misfit)
    return update(me.astype(jnp.int32).reshape(1), coef, modes, others, base_fields)


def solution(mesh):
    placed = (
        P("slab", None, None),
        P("slab", None, None),
        P("mode", "slab", None, None),
        P("slab"),
        P("slab"),
        P("slab", None),
        P(None, "slab", "mode", None),
    )
    return jax.shard_map(
        on_device,
        mesh=mesh,
        in_specs=placed,
        out_specs=P(None, "slab", "mode", None),
        check_vma=False,
    )
```

```python
import functools
import math

import jax
import jax.numpy as jnp
from jax import lax
from jax.experimental import pallas as pl
from jax.experimental.pallas import tpu as pltpu
from jax.sharding import PartitionSpec as P

ITERS = 3
STORAGE = 0.05
REACH = ITERS - 1
MIB = 1 << 20
ROWS = 8


def sweep_weights(count):
    order = []
    low, high = (0, count - 1)
    while low <= high:
        order.append(low)
        if high != low:
            order.append(high)
        low += 1
        high -= 1
    return [1.0 / (1.15 + 0.85 * math.cos((2 * i + 1) * math.pi / (2 * count))) for i in order]


W0, W1, W2 = sweep_weights(ITERS)
SCALE_B = W0 * W1
SCALE_A = (1.0 - W1) * W0 + W1
SELF_2 = SCALE_A / SCALE_B
SELF_3 = (1.0 - W2) / W2
SOURCE_3 = 1.0 / SCALE_B


def stencil_kernel(
    planes, width, modes_count, group, n_slab, plan_ref,
    log_ref, slope_ref, modes_ref, own_ref, below_ref, above_ref,
    coef, gain, cond, t_ref, u_ref, r_ref,
):
    step = pl.program_id(0)
    lanes = log_ref.shape[-1]
    pad = 8
    tiles = width // 8
    stride = pick_stride(modes_count)
    n_ext = planes + 2 * REACH + 2
    first = lax.axis_index("slab") == 0
    last = lax.axis_index("slab") == n_slab - 1

    @pl.when(step == 0)
    def _():
        cond[...] = jnp.ones_like(cond)
        for z in range(n_ext):
            cond[pl.ds(pad + z * width, width), :] = jnp.exp(log_ref[z])

        @pl.when(first)
        def _():
            cond[pl.ds(pad + 2 * width, width), :] = cond[pl.ds(pad + 3 * width, width), :]

        @pl.when(last)
        def _():
            cond[pl.ds(pad + (planes + 3) * width, width), :] = cond[
                pl.ds(pad + (planes + 2) * width, width), :
            ]

        t_ref[...] = jnp.zeros_like(t_ref)
        u_ref[...] = jnp.zeros_like(u_ref)
        rows = lax.broadcasted_iota(jnp.int32, (8, lanes), 0)
        cols = lax.broadcasted_iota(jnp.int32, (8, lanes), 1)
        for z in range(planes + 2 * REACH):
            def body(i, carry, z=z):
                at = pad + (z + 1) * width + i * 8
                c = cond[pl.ds(at, 8), :]

                def harmonic(other):
                    return 2.0 * c * other / (c + other)

                x = rows + i * 8
                lower = harmonic(cond[pl.ds(at - width, 8), :])
                upper = harmonic(cond[pl.ds(at + width, 8), :])
                west = harmonic(jnp.where(x == 0, c, cond[pl.ds(at - 1, 8), :]))
                east = harmonic(jnp.where(x == width - 1, c, cond[pl.ds(at + 1, 8), :]))
                south = harmonic(jnp.where(cols == 0, c, pltpu.roll(c, 1, axis=1)))
                north = harmonic(jnp.where(cols == lanes - 1, c, pltpu.roll(c, lanes - 1, axis=1)))
                inverse = 1.0 / (STORAGE + lower + upper + west + east + south + north)
                zero = jnp.zeros_like(c)
                if z < REACH:
                    upper = jnp.where(first, zero, upper)
                if z == REACH:
                    lower = jnp.where(first, zero, lower)
                if z == REACH + planes - 1:
                    upper = jnp.where(last, zero, upper)
                if z >= REACH + planes:
                    lower = jnp.where(last, zero, lower)
                here = pl.ds(i * 8, 8)
                coef[z, 0, here, :] = lower * inverse
                coef[z, 1, here, :] = upper * inverse
                coef[z, 2, here, :] = jnp.where(x == 0, zero, west * inverse)
                coef[z, 3, here, :] = jnp.where(x == width - 1, zero, east * inverse)
                coef[z, 4, here, :] = jnp.where(cols == 0, zero, south * inverse)
                coef[z, 5, here, :] = jnp.where(cols == lanes - 1, zero, north * inverse)
                if REACH <= z < REACH + planes:
                    gain[z - REACH, here, :] = (
                        (W2 * SCALE_B) * slope_ref[z - REACH, here, :] * c * inverse
                    )
                return carry

            lax.fori_loop(0, tiles, body, 0, unroll=8)
        r_ref[pl.ds((planes + 2 * REACH) * width * stride, modes_count), :] = jnp.zeros(
            (modes_count, lanes), jnp.float32
        )

    for z in range(planes):
        def convert(i, carry, z=z):
            here = pl.ds(i * 16, 16)
            g = gain[z, here, :]
            for m in range(group):
                t_ref[m, pl.ds(pad + z * width + i * 16, 16), :] = g * modes_ref[
                    m, z, here, :
                ].astype(jnp.float32)
            return carry

        lax.fori_loop(0, width // 16, convert, 0, unroll=8)

    def beside(ref, m, at, c, terms):
        total = None
        centre = ref[m, pl.ds(at, 8), :]
        for name in terms:
            if name == 0:
                v = ref[m, pl.ds(at - width, 8), :]
            elif name == 1:
                v = ref[m, pl.ds(at + width, 8), :]
            elif name == 2:
                v = ref[m, pl.ds(at - 1, 8), :]
            elif name == 3:
                v = ref[m, pl.ds(at + 1, 8), :]
            elif name == 4:
                v = pltpu.roll(centre, 1, axis=1)
            else:
                v = pltpu.roll(centre, lanes - 1, axis=1)
            v = c[name] * v
            total = v if total is None else total + v
        return centre, total

    for z in range(-1, planes + 1):
        if z == -1:
            terms = (1,)
        elif z == planes:
            terms = (0,)
        else:
            terms = (2, 3, 4, 5) + ((0,) if z > 0 else ()) + ((1,) if z < planes - 1 else ())

        def second(i, carry, z=z, terms=terms):
            c = {n: coef[z + REACH, n, pl.ds(i * 8, 8), :] for n in terms}
            at = pad + z * width + i * 8
            put = pl.ds(pad + (z + 1) * width + i * 8, 8)
            for m in range(group):
                if 0 <= z < planes:
                    centre, total = beside(t_ref, m, at, c, terms)
                    total = total + SELF_2 * centre
                elif z == -1:
                    total = c[1] * t_ref[m, pl.ds(at + width, 8), :]
                else:
                    total = c[0] * t_ref[m, pl.ds(at - width, 8), :]
                u_ref[m, put, :] = total
            return carry

        lax.fori_loop(0, tiles, second, 0, unroll=tiles)

    for z in range(-2, planes + 2):
        if z == -2:
            terms = (1,)
        elif z == planes + 1:
            terms = (0,)
        else:
            terms = (2, 3, 4, 5) + ((0,) if z > -1 else ()) + ((1,) if z < planes else ())

        def third(i, carry, z=z, terms=terms):
            c = {n: coef[z + REACH, n, pl.ds(i * 8, 8), :] for n in terms}
            at = pad + (z + 1) * width + i * 8
            for m in range(group):
                if z == -2:
                    total = c[1] * u_ref[m, pl.ds(at + width, 8), :]
                elif z == planes + 1:
                    total = c[0] * u_ref[m, pl.ds(at - width, 8), :]
                else:
                    centre, total = beside(u_ref, m, at, c, terms)
                    total = total + SELF_3 * centre
                    if 0 <= z < planes:
                        total = total + SOURCE_3 * t_ref[m, pl.ds(pad + z * width + i * 8, 8), :]
                put = ((z + REACH) * width + i * 8) * stride + step * group + m
                r_ref[pl.ds(put, 8, stride=stride), :] = total
            return carry

        lax.fori_loop(0, tiles, third, 0, unroll=tiles)

    @pl.when(step == pl.num_programs(0) - 1)
    def _():
        cols = lax.broadcasted_iota(jnp.int32, (modes_count, lanes), 1)
        blocks = plan_ref.shape[1]
        for kind, out in enumerate((own_ref, below_ref, above_ref)):

            def block(b, carry, kind=kind, out=out):
                def one(i, acc):
                    start = pl.multiple_of(plan_ref[2 * kind, b, i], 8)
                    v = r_ref[pl.ds(start, modes_count), :]
                    v = pltpu.roll(v, plan_ref[2 * kind + 1, b, i], axis=1)
                    return jnp.where(cols == i, v, acc)

                acc = lax.fori_loop(
                    0, lanes, one, jnp.zeros((modes_count, lanes), jnp.float32), unroll=lanes
                )
                out[:, pl.ds(pl.multiple_of(b * lanes, lanes), lanes)] = acc
                return carry

            lax.fori_loop(0, blocks, block, 0)


def pick_stride(modes_count):
    return 8 * (pl.cdiv(modes_count, 8) | 1)


def stencil(plan, log_ext, slope, modes):
    modes_count, planes, width, lanes = modes.shape
    count = plan.shape[1] * plan.shape[2]
    group = min(8, modes_count)
    n_ext = planes + 2 * REACH + 2
    stride = pick_stride(modes_count)
    smem = pl.BlockSpec(memory_space=pltpu.SMEM)
    vmem = pl.BlockSpec(memory_space=pltpu.VMEM)
    shape = jax.ShapeDtypeStruct((modes_count, count), jnp.float32)
    return pl.pallas_call(
        functools.partial(
            stencil_kernel, planes, width, modes_count, group, lax.axis_size("slab")
        ),
        grid=(modes_count // group,),
        out_shape=(shape, shape, shape),
        in_specs=[smem, vmem, vmem, pl.BlockSpec((group, planes, width, lanes), lambda s: (s, 0, 0, 0))],
        out_specs=(pl.BlockSpec((modes_count, count), lambda s: (0, 0)),) * 3,
        scratch_shapes=[
            pltpu.VMEM((planes + 2 * REACH, 6, width, lanes), jnp.float32),
            pltpu.VMEM((planes, width, lanes), jnp.float32),
            pltpu.VMEM((n_ext * width + 16, lanes), jnp.float32),
            pltpu.VMEM((group, planes * width + 16, lanes), jnp.float32),
            pltpu.VMEM((group, (planes + 2) * width + 16, lanes), jnp.float32),
            pltpu.VMEM(((planes + 2 * REACH) * width * stride + modes_count, lanes), jnp.float32),
        ],
        compiler_params=pltpu.CompilerParams(
            dimension_semantics=("arbitrary",), vmem_limit_bytes=61 * MIB
        ),
        cost_estimate=pl.CostEstimate(
            flops=40 * modes.size, bytes_accessed=4 * modes.size, transcendentals=0
        ),
        name="stencil",
    )(plan, log_ext, slope, modes)


def halo_kernel(n_mode, n_slab, stride, log_ref, cells_ref, modes_ref, ext, plan, *rest):
    pieces = rest[: n_mode - 1]
    cells_b, cells_a, send, recv, local = rest[n_mode - 1 :]
    me = lax.axis_index("mode")
    slab = lax.axis_index("slab")
    planes, width, lanes = log_ref.shape
    part = width // n_mode
    halo = REACH + 1
    has_below = slab > 0
    has_above = slab < n_slab - 1
    slab_up = jnp.minimum(slab + 1, n_slab - 1)
    slab_down = jnp.maximum(slab - 1, 0)
    barrier = pltpu.get_barrier_semaphore()

    @pl.when(jnp.logical_not(has_below))
    def _():
        ext[:halo] = jnp.zeros((halo, width, lanes), jnp.float32)
        cells_b[...] = jnp.zeros_like(cells_b)

    @pl.when(jnp.logical_not(has_above))
    def _():
        ext[halo + planes :] = jnp.zeros((halo, width, lanes), jnp.float32)
        cells_a[...] = jnp.zeros_like(cells_a)

    def greet(device):
        pl.semaphore_signal(barrier, inc=1, device_id=device, device_id_type=pl.DeviceIdType.MESH)

    @pl.when(has_above)
    def _():
        greet((me, slab_up))

    @pl.when(has_below)
    def _():
        greet((me, slab_down))

    moves = []
    for d in range(1, n_mode):
        to = lax.rem(me + d, n_mode)
        source = modes_ref.at[:, :, pl.ds(pl.multiple_of(to * part, 16), part), :]
        moves.append(pltpu.make_async_copy(source, pieces[d - 1], local.at[d]))
    pl.semaphore_wait(barrier, jnp.where(has_below, 1, 0) + jnp.where(has_above, 1, 0))

    def remote(src, dst, k, device):
        return pltpu.make_async_remote_copy(
            src_ref=src, dst_ref=dst, send_sem=send.at[k], recv_sem=recv.at[k],
            device_id=device, device_id_type=pl.DeviceIdType.MESH,
        )

    up = (
        remote(log_ref.at[planes - halo :], ext.at[:halo], 0, (me, slab_up)),
        remote(cells_ref, cells_b, 1, (me, slab_up)),
    )
    down = (
        remote(log_ref.at[:halo], ext.at[halo + planes :], 2, (me, slab_down)),
        remote(cells_ref, cells_a, 3, (me, slab_down)),
    )

    @pl.when(has_above)
    def _():
        for copy in up:
            copy.start()

    @pl.when(has_below)
    def _():
        for copy in down:
            copy.start()

    for move in moves:
        move.start()
    ext[halo : halo + planes] = log_ref[...]

    @pl.when(has_below)
    def _():
        for copy in up:
            copy.wait_recv()

    @pl.when(has_above)
    def _():
        for copy in down:
            copy.wait_recv()

    column = lax.broadcasted_iota(jnp.int32, cells_ref.shape, 1)
    zero_row = (planes + 2 * REACH) * width
    for kind, (cells, low, high, offset) in enumerate(
        (
            (cells_ref, 0, planes, REACH),
            (cells_b, planes - REACH, planes, REACH - planes),
            (cells_a, 0, REACH, REACH + planes),
        )
    ):
        cell = cells[...]
        row = cell // lanes
        inside = jnp.logical_and(row >= low * width, row < high * width)
        row = jnp.where(inside, row + offset * width, zero_row)
        plan[2 * kind] = row * stride
        plan[2 * kind + 1] = lax.rem(column - (cell - cell // lanes * lanes) + lanes, lanes)

    @pl.when(has_above)
    def _():
        for copy in up:
            copy.wait_send()

    @pl.when(has_below)
    def _():
        for copy in down:
            copy.wait_send()

    for move in moves:
        move.wait()


def halo(log_cond, obs_cells, modes):
    planes, width, lanes = log_cond.shape
    modes_count = modes.shape[0]
    n_mode = lax.axis_size("mode")
    n_slab = lax.axis_size("slab")
    cells = obs_cells.reshape(-1, lanes)
    vmem = pl.BlockSpec(memory_space=pltpu.VMEM)
    hbm = pl.BlockSpec(memory_space=pl.ANY)
    dma = pltpu.SemaphoreType.DMA
    piece = jax.ShapeDtypeStruct((modes_count, planes, width // n_mode, lanes), modes.dtype)
    return pl.pallas_call(
        functools.partial(halo_kernel, n_mode, n_slab, pick_stride(modes_count)),
        out_shape=(
            jax.ShapeDtypeStruct((planes + 2 * REACH + 2, width, lanes), jnp.float32),
            jax.ShapeDtypeStruct((6,) + cells.shape, jnp.int32),
        )
        + (piece,) * (n_mode - 1),
        in_specs=[vmem, vmem, hbm],
        out_specs=(vmem, vmem) + (hbm,) * (n_mode - 1),
        scratch_shapes=[
            pltpu.VMEM(cells.shape, jnp.int32),
            pltpu.VMEM(cells.shape, jnp.int32),
            dma((4,)), dma((4,)), dma((n_mode,)),
        ],
        compiler_params=pltpu.CompilerParams(
            collective_id=1, has_side_effects=True, vmem_limit_bytes=61 * MIB
        ),
        name="halo",
    )(log_cond, cells, modes)


def eliminate(matrix, n, block=4):
    tall = lax.broadcasted_iota(jnp.int32, matrix.shape, 0)
    for start in range(0, n, block):
        columns = [
            jnp.broadcast_to(matrix[:, j : j + 1], matrix.shape)
            for j in range(start, start + block)
        ]
        for i in range(block):
            j = start + i
            inverse = 1.0 / columns[i][j : j + 1, :]
            at = tall == j
            row = matrix[j : j + 1, :] * inverse
            matrix = jnp.where(at, row, matrix - columns[i] * row)
            for k in range(i + 1, block):
                entry = columns[k][j : j + 1, :] * inverse
                columns[k] = jnp.where(at, entry, columns[k] - columns[i] * entry)
    return matrix


def stages_of(n_mode, n_slab):
    stages = []
    stride = 1
    while stride < n_slab:
        radix = next(r for r in (4, 2, 3, n_slab // stride) if (n_slab // stride) % r == 0)
        stages.append((n_mode if stride == 1 else 1, stride, radix))
        stride *= radix
    return stages or [(n_mode, 1, 1)]


def reduce_kernel(
    n_mode, n_slab, stages, own, below, above, var, miss, out,
    in_b, in_a, picked, whole, sums, work,
    halo_send, halo_recv, mode_send, mode_recv, sum_send, sum_recv,
):
    me = lax.axis_index("mode")
    slab = lax.axis_index("slab")
    mine, count = own.shape
    split = count // n_mode
    n = mine * n_mode
    f = miss.shape[0]
    has_below = slab > 0
    has_above = slab < n_slab - 1
    slab_up = jnp.minimum(slab + 1, n_slab - 1)
    slab_down = jnp.maximum(slab - 1, 0)

    def member(stage, d):
        modes, stride, radix = stage
        low = lax.rem(slab // stride, radix)
        if modes == 1:
            return me, slab + (lax.rem(low + d, radix) - low) * stride
        g = lax.rem(me * radix + low + d, modes * radix)
        return g // radix, slab + (lax.rem(g, radix) - low) * stride

    @pl.when(jnp.logical_not(has_below))
    def _():
        in_b[...] = jnp.zeros_like(in_b)

    @pl.when(jnp.logical_not(has_above))
    def _():
        in_a[...] = jnp.zeros_like(in_a)

    barrier = pltpu.get_barrier_semaphore()

    def greet(device):
        pl.semaphore_signal(barrier, inc=1, device_id=device, device_id_type=pl.DeviceIdType.MESH)

    @pl.when(has_above)
    def _():
        greet((me, slab_up))

    @pl.when(has_below)
    def _():
        greet((me, slab_down))

    greeted = 0
    for d in range(1, n_mode):
        greet((lax.rem(me + d, n_mode), slab))
        greeted += 1
    for stage in stages:
        for d in range(1, stage[0] * stage[2]):
            greet(member(stage, d))
            greeted += 1
    ends = jnp.where(has_below, 1, 0) + jnp.where(has_above, 1, 0)
    pl.semaphore_wait(barrier, greeted + ends)

    def remote(src, dst, send, recv, device):
        return pltpu.make_async_remote_copy(
            src_ref=src, dst_ref=dst, send_sem=send, recv_sem=recv,
            device_id=device, device_id_type=pl.DeviceIdType.MESH,
        )

    pieces = []
    for d in range(n_mode):
        to = lax.rem(me + d, n_mode)
        pieces.append(pl.ds(pl.multiple_of(to * split, 128), split))
    going_up = [
        remote(above.at[:, p], in_b.at[:, p], halo_send.at[d], halo_recv.at[d], (me, slab_up))
        for d, p in enumerate(pieces)
    ]
    going_down = [
        remote(below.at[:, p], in_a.at[:, p], halo_send.at[n_mode + d], halo_recv.at[n_mode + d],
               (me, slab_down))
        for d, p in enumerate(pieces)
    ]
    order = list(range(1, n_mode)) + [0]
    for d in order:

        @pl.when(has_above)
        def _(d=d):
            going_up[d].start()

        @pl.when(has_below)
        def _(d=d):
            going_down[d].start()

    copies = []
    for d in order:

        @pl.when(has_below)
        def _(d=d):
            going_up[d].wait_recv()

        @pl.when(has_above)
        def _(d=d):
            going_down[d].wait_recv()

        p = pieces[d]
        total = own[:, p] + in_b[:, p] + in_a[:, p]
        if d:
            picked[:, p] = total
            to = lax.rem(me + d, n_mode)
            copies.append(
                remote(picked.at[:, p], whole.at[me], mode_send.at[d], mode_recv.at[d], (to, slab))
            )
            copies[-1].start()
        else:
            whole[me] = total
    here = pieces[0]
    for copy in copies:
        copy.wait_recv()
    every = whole[...].reshape(n, split)
    scaled = every / var[:, here]
    gram = lax.dot_general(
        scaled, every, (((1,), (1,)), ((), ())), precision=lax.Precision.HIGHEST,
        preferred_element_type=jnp.float32,
    )
    rhs = lax.dot_general(
        miss[:, here], scaled, (((1,), (1,)), ((), ())), precision=lax.Precision.HIGHEST,
        preferred_element_type=jnp.float32,
    )
    top, some = n // 2, f // 2
    sums[0, :top, :n] = gram[:top]
    sums[0, :top, n:] = gram[top:]
    sums[0, top:, :n] = rhs[:some]
    sums[0, top:, n:] = rhs[some:]

    base = 0
    sem = 0
    for stage in stages:
        size = stage[0] * stage[2]
        if base:
            sums[base] = total
        moving = []
        for d in range(1, size):
            moving.append(
                remote(sums.at[base], sums.at[base + d], sum_send.at[sem], sum_recv.at[sem],
                       member(stage, d))
            )
            moving[-1].start()
            sem += 1
        low = lax.rem(slab // stage[1], stage[2])
        if stage[0] > 1:
            low = low + me * stage[2]
        for copy in moving:
            copy.wait_recv()
        total = None
        for q in range(size):
            term = sums[base + lax.rem(low - q + size, size)]
            total = term if total is None else total + term
        copies += moving
        base += size

    work[...] = jnp.zeros_like(work)
    work[:top, :n] = total[:top, :n]
    work[top:n, :n] = total[:top, n:]
    work[n : n + some, :n] = total[top:, :n]
    work[n + some : n + f, :n] = total[top:, n:]
    matrix = work[...].T[:n]
    tall = lax.broadcasted_iota(jnp.int32, matrix.shape, 0)
    wide = lax.broadcasted_iota(jnp.int32, matrix.shape, 1)
    work[:n] = eliminate(matrix + jnp.where(tall == wide, 1.0, 0.0), n)
    for d in range(n_mode):
        block = lax.rem(me - d + n_mode, n_mode)
        out[d * mine : (d + 1) * mine, :] = work[
            pl.ds(pl.multiple_of(block * mine, 8), mine), n : n + f
        ]

    @pl.when(has_above)
    def _():
        for copy in going_up:
            copy.wait_send()

    @pl.when(has_below)
    def _():
        for copy in going_down:
            copy.wait_send()

    for copy in copies:
        copy.wait_send()


def reduce_and_solve(own, below, above, obs_var, misfit):
    n_mode = lax.axis_size("mode")
    n_slab = lax.axis_size("slab")
    mine, count = own.shape
    n = mine * n_mode
    f = misfit.shape[1]
    stages = stages_of(n_mode, n_slab)
    slots = sum(s[0] * s[2] for s in stages)
    wide = 128 * pl.cdiv(n + f, 128)
    vmem = pl.BlockSpec(memory_space=pltpu.VMEM)
    dma = pltpu.SemaphoreType.DMA
    return pl.pallas_call(
        functools.partial(reduce_kernel, n_mode, n_slab, stages),
        out_shape=jax.ShapeDtypeStruct((n, f), jnp.float32),
        in_specs=[vmem] * 5,
        out_specs=vmem,
        scratch_shapes=[
            pltpu.VMEM((mine, count), jnp.float32),
            pltpu.VMEM((mine, count), jnp.float32),
            pltpu.VMEM((mine, count), jnp.float32),
            pltpu.VMEM((n_mode, mine, count // n_mode), jnp.float32),
            pltpu.VMEM((slots, (n + f) // 2, 2 * n), jnp.float32),
            pltpu.VMEM((wide, wide), jnp.float32),
            dma((2 * n_mode,)), dma((2 * n_mode,)), dma((n_mode,)), dma((n_mode,)), dma((slots,)), dma((slots,)),
        ],
        compiler_params=pltpu.CompilerParams(
            collective_id=0, has_side_effects=True, vmem_limit_bytes=24 * MIB
        ),
        cost_estimate=pl.CostEstimate(
            flops=2 * n * n * count, bytes_accessed=1 << 20, transcendentals=0
        ),
        name="reduce_and_solve",
    )(own, below, above, obs_var.reshape(1, count), misfit.T)


def update_kernel(place_ref, coef_ref, own_ref, others_ref, base_ref, out_ref, big):
    fields, deep, rows, lanes = out_ref.shape
    total = coef_ref.shape[0]
    mine = own_ref.shape[0]

    @pl.when(jnp.logical_and(pl.program_id(0) == 0, pl.program_id(1) == 0))
    def _():
        coef = coef_ref[...]
        high = coef.astype(jnp.bfloat16)
        low = (coef - high.astype(jnp.float32)).astype(jnp.bfloat16)
        tall, wide = fields * ROWS, total * ROWS
        r0 = lax.broadcasted_iota(jnp.int32, (tall, fields), 0)
        f0 = lax.broadcasted_iota(jnp.int32, (tall, fields), 1)
        spread_f = jnp.where(r0 // ROWS == f0, 1.0, 0.0).astype(jnp.bfloat16)
        k0 = lax.broadcasted_iota(jnp.int32, (total, wide), 0)
        c0 = lax.broadcasted_iota(jnp.int32, (total, wide), 1)
        spread_k = jnp.where(c0 // ROWS == k0, 1.0, 0.0).astype(jnp.bfloat16)
        r1 = lax.broadcasted_iota(jnp.int32, (tall, wide), 0)
        c1 = lax.broadcasted_iota(jnp.int32, (tall, wide), 1)
        same = r1 % ROWS == c1 % ROWS
        for p, part in enumerate((high, low)):
            a = lax.dot_general(
                spread_f, part, (((1,), (1,)), ((), ())), preferred_element_type=jnp.float32
            ).astype(jnp.bfloat16)
            b = jnp.dot(a, spread_k, preferred_element_type=jnp.float32)
            big[p * tall : (p + 1) * tall, :] = jnp.where(same, b, 0.0).astype(jnp.bfloat16)

    tall = fields * ROWS
    left = mine * ROWS

    def side(ref):
        count = ref.shape[0]
        tiles = []
        for d in range(deep):
            whole = ref[:, d].astype(jnp.float32)
            for h in range(rows // ROWS):
                tile = whole[:, h * ROWS : (h + 1) * ROWS, :]
                tiles.append(tile.reshape(count * ROWS, lanes).astype(jnp.bfloat16))
        return jnp.concatenate(tiles, axis=1)

    both = jnp.dot(big[:, :left], side(own_ref), preferred_element_type=jnp.float32)
    both = both + jnp.dot(big[:, left:], side(others_ref), preferred_element_type=jnp.float32)
    both = both[:tall] + both[tall:]
    for d in range(deep):
        base = base_ref[:, d].astype(jnp.float32)
        for h in range(rows // ROWS):
            at = (d * (rows // ROWS) + h) * lanes
            part = both[:, at : at + lanes].reshape(fields, ROWS, lanes)
            out_ref[:, d, h * ROWS : (h + 1) * ROWS, :] = (
                base[:, h * ROWS : (h + 1) * ROWS, :] + part
            )


def update(place, coef, modes, others, base):
    fields, planes, width, lanes = base.shape
    mine = modes.shape[0]
    rest = others.shape[0]
    rows = 16
    deep = 2
    steps = width // rows

    def fixed(count):
        return pl.BlockSpec((count, deep, rows, lanes), lambda z, x, place: (0, z, x, 0))

    return pl.pallas_call(
        update_kernel,
        grid_spec=pltpu.PrefetchScalarGridSpec(
            num_scalar_prefetch=1,
            grid=(planes // deep, steps),
            in_specs=[
                pl.BlockSpec(coef.shape, lambda z, x, place: (0, 0)),
                pl.BlockSpec(
                    (mine, deep, rows, lanes),
                    lambda z, x, place: (0, z, place[0] * steps + x, 0),
                ),
                fixed(rest),
                fixed(fields),
            ],
            out_specs=fixed(fields),
            scratch_shapes=[
                pltpu.VMEM((2 * fields * ROWS, (mine + rest) * ROWS), jnp.bfloat16)
            ],
        ),
        out_shape=jax.ShapeDtypeStruct(base.shape, jnp.float32),
        compiler_params=pltpu.CompilerParams(
            dimension_semantics=("arbitrary", "arbitrary"), vmem_limit_bytes=61 * MIB
        ),
        name="update",
    )(place, coef, modes, others, base)


def on_device(log_cond, head_slope, modes, obs_cells, obs_var, misfit, base_fields):
    n_mode = lax.axis_size("mode")
    me = lax.axis_index("mode")
    log_ext, plan, *pieces = halo(log_cond, obs_cells, modes)
    received = [
        lax.ppermute(piece, "mode", [(i, (i + d) % n_mode) for i in range(n_mode)])
        for d, piece in enumerate(pieces, 1)
    ]
    others = received[0] if n_mode == 2 else jnp.concatenate(received, axis=0)
    own, below, above = stencil(plan, log_ext, head_slope, modes)
    coef = reduce_and_solve(own, below, above, obs_var, misfit)
    return update(me.astype(jnp.int32).reshape(1), coef, modes, others, base_fields)


def solution(mesh):
    placed = (
        P("slab", None, None),
        P("slab", None, None),
        P("mode", "slab", None, None),
        P("slab"),
        P("slab"),
        P("slab", None),
        P(None, "slab", "mode", None),
    )
    return jax.shard_map(
        on_device,
        mesh=mesh,
        in_specs=placed,
        out_specs=P(None, "slab", "mode", None),
        check_vma=False,
    )
```

```python
import functools
import math

import jax
import jax.numpy as jnp
from jax import lax
from jax.experimental import pallas as pl
from jax.experimental.pallas import tpu as pltpu
from jax.sharding import PartitionSpec as P

ITERS = 3
STORAGE = 0.05
REACH = ITERS - 1
MIB = 1 << 20
ROWS = 8


def sweep_weights(count):
    order = []
    low, high = (0, count - 1)
    while low <= high:
        order.append(low)
        if high != low:
            order.append(high)
        low += 1
        high -= 1
    return [1.0 / (1.15 + 0.85 * math.cos((2 * i + 1) * math.pi / (2 * count))) for i in order]


W0, W1, W2 = sweep_weights(ITERS)
SCALE_B = W0 * W1
SCALE_A = (1.0 - W1) * W0 + W1
SELF_2 = SCALE_A / SCALE_B
SELF_3 = (1.0 - W2) / W2
SOURCE_3 = 1.0 / SCALE_B


def stencil_kernel(
    planes, width, modes_count, group, n_slab, plan_ref,
    log_ref, slope_ref, modes_ref, own_ref, below_ref, above_ref,
    coef, gain, cond, t_ref, u_ref, r_ref,
):
    step = pl.program_id(0)
    lanes = log_ref.shape[-1]
    pad = 8
    tiles = width // 8
    stride = pick_stride(modes_count)
    n_ext = planes + 2 * REACH + 2
    first = lax.axis_index("slab") == 0
    last = lax.axis_index("slab") == n_slab - 1

    @pl.when(step == 0)
    def _():
        cond[...] = jnp.ones_like(cond)
        for z in range(n_ext):
            cond[pl.ds(pad + z * width, width), :] = jnp.exp(log_ref[z])

        @pl.when(first)
        def _():
            cond[pl.ds(pad + 2 * width, width), :] = cond[pl.ds(pad + 3 * width, width), :]

        @pl.when(last)
        def _():
            cond[pl.ds(pad + (planes + 3) * width, width), :] = cond[
                pl.ds(pad + (planes + 2) * width, width), :
            ]

        t_ref[...] = jnp.zeros_like(t_ref)
        u_ref[...] = jnp.zeros_like(u_ref)
        rows = lax.broadcasted_iota(jnp.int32, (8, lanes), 0)
        cols = lax.broadcasted_iota(jnp.int32, (8, lanes), 1)
        for z in range(planes + 2 * REACH):
            def body(i, carry, z=z):
                at = pad + (z + 1) * width + i * 8
                c = cond[pl.ds(at, 8), :]

                def harmonic(other):
                    return 2.0 * c * other / (c + other)

                x = rows + i * 8
                lower = harmonic(cond[pl.ds(at - width, 8), :])
                upper = harmonic(cond[pl.ds(at + width, 8), :])
                west = harmonic(jnp.where(x == 0, c, cond[pl.ds(at - 1, 8), :]))
                east = harmonic(jnp.where(x == width - 1, c, cond[pl.ds(at + 1, 8), :]))
                south = harmonic(jnp.where(cols == 0, c, pltpu.roll(c, 1, axis=1)))
                north = harmonic(jnp.where(cols == lanes - 1, c, pltpu.roll(c, lanes - 1, axis=1)))
                inverse = 1.0 / (STORAGE + lower + upper + west + east + south + north)
                zero = jnp.zeros_like(c)
                if z < REACH:
                    upper = jnp.where(first, zero, upper)
                if z == REACH:
                    lower = jnp.where(first, zero, lower)
                if z == REACH + planes - 1:
                    upper = jnp.where(last, zero, upper)
                if z >= REACH + planes:
                    lower = jnp.where(last, zero, lower)
                here = pl.ds(i * 8, 8)
                coef[z, 0, here, :] = lower * inverse
                coef[z, 1, here, :] = upper * inverse
                coef[z, 2, here, :] = jnp.where(x == 0, zero, west * inverse)
                coef[z, 3, here, :] = jnp.where(x == width - 1, zero, east * inverse)
                coef[z, 4, here, :] = jnp.where(cols == 0, zero, south * inverse)
                coef[z, 5, here, :] = jnp.where(cols == lanes - 1, zero, north * inverse)
                if REACH <= z < REACH + planes:
                    gain[z - REACH, here, :] = (
                        (W2 * SCALE_B) * slope_ref[z - REACH, here, :] * c * inverse
                    )
                return carry

            lax.fori_loop(0, tiles, body, 0, unroll=8)
        r_ref[pl.ds((planes + 2 * REACH) * width * stride, modes_count), :] = jnp.zeros(
            (modes_count, lanes), jnp.float32
        )

    for z in range(planes):
        def convert(i, carry, z=z):
            here = pl.ds(i * 16, 16)
            g = gain[z, here, :]
            for m in range(group):
                t_ref[m, pl.ds(pad + z * width + i * 16, 16), :] = g * modes_ref[
                    m, z, here, :
                ].astype(jnp.float32)
            return carry

        lax.fori_loop(0, width // 16, convert, 0, unroll=8)

    def beside(ref, m, at, c, terms):
        total = None
        centre = ref[m, pl.ds(at, 8), :]
        for name in terms:
            if name == 0:
                v = ref[m, pl.ds(at - width, 8), :]
            elif name == 1:
                v = ref[m, pl.ds(at + width, 8), :]
            elif name == 2:
                v = ref[m, pl.ds(at - 1, 8), :]
            elif name == 3:
                v = ref[m, pl.ds(at + 1, 8), :]
            elif name == 4:
                v = pltpu.roll(centre, 1, axis=1)
            else:
                v = pltpu.roll(centre, lanes - 1, axis=1)
            v = c[name] * v
            total = v if total is None else total + v
        return centre, total

    for z in range(-1, planes + 1):
        if z == -1:
            terms = (1,)
        elif z == planes:
            terms = (0,)
        else:
            terms = (2, 3, 4, 5) + ((0,) if z > 0 else ()) + ((1,) if z < planes - 1 else ())

        def second(i, carry, z=z, terms=terms):
            c = {n: coef[z + REACH, n, pl.ds(i * 8, 8), :] for n in terms}
            at = pad + z * width + i * 8
            put = pl.ds(pad + (z + 1) * width + i * 8, 8)
            for m in range(group):
                if 0 <= z < planes:
                    centre, total = beside(t_ref, m, at, c, terms)
                    total = total + SELF_2 * centre
                elif z == -1:
                    total = c[1] * t_ref[m, pl.ds(at + width, 8), :]
                else:
                    total = c[0] * t_ref[m, pl.ds(at - width, 8), :]
                u_ref[m, put, :] = total
            return carry

        lax.fori_loop(0, tiles, second, 0, unroll=tiles)

    for z in range(-2, planes + 2):
        if z == -2:
            terms = (1,)
        elif z == planes + 1:
            terms = (0,)
        else:
            terms = (2, 3, 4, 5) + ((0,) if z > -1 else ()) + ((1,) if z < planes else ())

        def third(i, carry, z=z, terms=terms):
            c = {n: coef[z + REACH, n, pl.ds(i * 8, 8), :] for n in terms}
            at = pad + (z + 1) * width + i * 8
            for m in range(group):
                if z == -2:
                    total = c[1] * u_ref[m, pl.ds(at + width, 8), :]
                elif z == planes + 1:
                    total = c[0] * u_ref[m, pl.ds(at - width, 8), :]
                else:
                    centre, total = beside(u_ref, m, at, c, terms)
                    total = total + SELF_3 * centre
                    if 0 <= z < planes:
                        total = total + SOURCE_3 * t_ref[m, pl.ds(pad + z * width + i * 8, 8), :]
                put = ((z + REACH) * width + i * 8) * stride + step * group + m
                r_ref[pl.ds(put, 8, stride=stride), :] = total
            return carry

        lax.fori_loop(0, tiles, third, 0, unroll=tiles)

    @pl.when(step == pl.num_programs(0) - 1)
    def _():
        cols = lax.broadcasted_iota(jnp.int32, (modes_count, lanes), 1)
        blocks = plan_ref.shape[1]
        for kind, out in enumerate((own_ref, below_ref, above_ref)):

            def block(b, carry, kind=kind, out=out):
                def one(i, acc):
                    start = pl.multiple_of(plan_ref[2 * kind, b, i], 8)
                    v = r_ref[pl.ds(start, modes_count), :]
                    v = pltpu.roll(v, plan_ref[2 * kind + 1, b, i], axis=1)
                    return jnp.where(cols == i, v, acc)

                acc = lax.fori_loop(
                    0, lanes, one, jnp.zeros((modes_count, lanes), jnp.float32), unroll=lanes
                )
                out[:, pl.ds(pl.multiple_of(b * lanes, lanes), lanes)] = acc
                return carry

            lax.fori_loop(0, blocks, block, 0)


def pick_stride(modes_count):
    return 8 * (pl.cdiv(modes_count, 8) | 1)


def stencil(plan, log_ext, slope, modes):
    modes_count, planes, width, lanes = modes.shape
    count = plan.shape[1] * plan.shape[2]
    group = min(8, modes_count)
    n_ext = planes + 2 * REACH + 2
    stride = pick_stride(modes_count)
    smem = pl.BlockSpec(memory_space=pltpu.SMEM)
    vmem = pl.BlockSpec(memory_space=pltpu.VMEM)
    shape = jax.ShapeDtypeStruct((modes_count, count), jnp.float32)
    return pl.pallas_call(
        functools.partial(
            stencil_kernel, planes, width, modes_count, group, lax.axis_size("slab")
        ),
        grid=(modes_count // group,),
        out_shape=(shape, shape, shape),
        in_specs=[smem, vmem, vmem, pl.BlockSpec((group, planes, width, lanes), lambda s: (s, 0, 0, 0))],
        out_specs=(pl.BlockSpec((modes_count, count), lambda s: (0, 0)),) * 3,
        scratch_shapes=[
            pltpu.VMEM((planes + 2 * REACH, 6, width, lanes), jnp.float32),
            pltpu.VMEM((planes, width, lanes), jnp.float32),
            pltpu.VMEM((n_ext * width + 16, lanes), jnp.float32),
            pltpu.VMEM((group, planes * width + 16, lanes), jnp.float32),
            pltpu.VMEM((group, (planes + 2) * width + 16, lanes), jnp.float32),
            pltpu.VMEM(((planes + 2 * REACH) * width * stride + modes_count, lanes), jnp.float32),
        ],
        compiler_params=pltpu.CompilerParams(
            dimension_semantics=("arbitrary",), vmem_limit_bytes=46 * MIB
        ),
        cost_estimate=pl.CostEstimate(
            flops=40 * modes.size, bytes_accessed=4 * modes.size, transcendentals=0
        ),
        name="stencil",
    )(plan, log_ext, slope, modes)


def halo_kernel(n_mode, n_slab, stride, log_ref, cells_ref, modes_ref, ext, plan, *rest):
    pieces = rest[: n_mode - 1]
    cells_b, cells_a, send, recv, local = rest[n_mode - 1 :]
    me = lax.axis_index("mode")
    slab = lax.axis_index("slab")
    planes, width, lanes = log_ref.shape
    part = width // n_mode
    halo = REACH + 1
    has_below = slab > 0
    has_above = slab < n_slab - 1
    slab_up = jnp.minimum(slab + 1, n_slab - 1)
    slab_down = jnp.maximum(slab - 1, 0)
    barrier = pltpu.get_barrier_semaphore()

    @pl.when(jnp.logical_not(has_below))
    def _():
        ext[:halo] = jnp.zeros((halo, width, lanes), jnp.float32)
        cells_b[...] = jnp.zeros_like(cells_b)

    @pl.when(jnp.logical_not(has_above))
    def _():
        ext[halo + planes :] = jnp.zeros((halo, width, lanes), jnp.float32)
        cells_a[...] = jnp.zeros_like(cells_a)

    def greet(device):
        pl.semaphore_signal(barrier, inc=1, device_id=device, device_id_type=pl.DeviceIdType.MESH)

    @pl.when(has_above)
    def _():
        greet((me, slab_up))

    @pl.when(has_below)
    def _():
        greet((me, slab_down))

    moves = []
    for d in range(1, n_mode):
        to = lax.rem(me + d, n_mode)
        source = modes_ref.at[:, :, pl.ds(pl.multiple_of(to * part, 16), part), :]
        moves.append(pltpu.make_async_copy(source, pieces[d - 1], local.at[d]))
    pl.semaphore_wait(barrier, jnp.where(has_below, 1, 0) + jnp.where(has_above, 1, 0))

    def remote(src, dst, k, device):
        return pltpu.make_async_remote_copy(
            src_ref=src, dst_ref=dst, send_sem=send.at[k], recv_sem=recv.at[k],
            device_id=device, device_id_type=pl.DeviceIdType.MESH,
        )

    up = (
        remote(log_ref.at[planes - halo :], ext.at[:halo], 0, (me, slab_up)),
        remote(cells_ref, cells_b, 1, (me, slab_up)),
    )
    down = (
        remote(log_ref.at[:halo], ext.at[halo + planes :], 2, (me, slab_down)),
        remote(cells_ref, cells_a, 3, (me, slab_down)),
    )

    @pl.when(has_above)
    def _():
        for copy in up:
            copy.start()

    @pl.when(has_below)
    def _():
        for copy in down:
            copy.start()

    for move in moves:
        move.start()
    ext[halo : halo + planes] = log_ref[...]

    @pl.when(has_below)
    def _():
        for copy in up:
            copy.wait_recv()

    @pl.when(has_above)
    def _():
        for copy in down:
            copy.wait_recv()

    column = lax.broadcasted_iota(jnp.int32, cells_ref.shape, 1)
    zero_row = (planes + 2 * REACH) * width
    for kind, (cells, low, high, offset) in enumerate(
        (
            (cells_ref, 0, planes, REACH),
            (cells_b, planes - REACH, planes, REACH - planes),
            (cells_a, 0, REACH, REACH + planes),
        )
    ):
        cell = cells[...]
        row = cell // lanes
        inside = jnp.logical_and(row >= low * width, row < high * width)
        row = jnp.where(inside, row + offset * width, zero_row)
        plan[2 * kind] = row * stride
        plan[2 * kind + 1] = lax.rem(column - (cell - cell // lanes * lanes) + lanes, lanes)

    @pl.when(has_above)
    def _():
        for copy in up:
            copy.wait_send()

    @pl.when(has_below)
    def _():
        for copy in down:
            copy.wait_send()

    for move in moves:
        move.wait()


def halo(log_cond, obs_cells, modes):
    planes, width, lanes = log_cond.shape
    modes_count = modes.shape[0]
    n_mode = lax.axis_size("mode")
    n_slab = lax.axis_size("slab")
    cells = obs_cells.reshape(-1, lanes)
    vmem = pl.BlockSpec(memory_space=pltpu.VMEM)
    hbm = pl.BlockSpec(memory_space=pl.ANY)
    dma = pltpu.SemaphoreType.DMA
    piece = jax.ShapeDtypeStruct((modes_count, planes, width // n_mode, lanes), modes.dtype)
    return pl.pallas_call(
        functools.partial(halo_kernel, n_mode, n_slab, pick_stride(modes_count)),
        out_shape=(
            jax.ShapeDtypeStruct((planes + 2 * REACH + 2, width, lanes), jnp.float32),
            jax.ShapeDtypeStruct((6,) + cells.shape, jnp.int32),
        )
        + (piece,) * (n_mode - 1),
        in_specs=[vmem, vmem, hbm],
        out_specs=(vmem, vmem) + (vmem,) * (n_mode - 1),
        scratch_shapes=[
            pltpu.VMEM(cells.shape, jnp.int32),
            pltpu.VMEM(cells.shape, jnp.int32),
            dma((4,)), dma((4,)), dma((n_mode,)),
        ],
        compiler_params=pltpu.CompilerParams(
            collective_id=1, has_side_effects=True, vmem_limit_bytes=61 * MIB
        ),
        name="halo",
    )(log_cond, cells, modes)


def eliminate(matrix, n, block=4):
    tall = lax.broadcasted_iota(jnp.int32, matrix.shape, 0)
    for start in range(0, n, block):
        columns = [
            jnp.broadcast_to(matrix[:, j : j + 1], matrix.shape)
            for j in range(start, start + block)
        ]
        for i in range(block):
            j = start + i
            inverse = 1.0 / columns[i][j : j + 1, :]
            at = tall == j
            row = matrix[j : j + 1, :] * inverse
            matrix = jnp.where(at, row, matrix - columns[i] * row)
            for k in range(i + 1, block):
                entry = columns[k][j : j + 1, :] * inverse
                columns[k] = jnp.where(at, entry, columns[k] - columns[i] * entry)
    return matrix


def stages_of(n_mode, n_slab):
    stages = []
    stride = 1
    while stride < n_slab:
        radix = next(r for r in (4, 2, 3, n_slab // stride) if (n_slab // stride) % r == 0)
        stages.append((n_mode if stride == 1 else 1, stride, radix))
        stride *= radix
    return stages or [(n_mode, 1, 1)]


def reduce_kernel(
    n_mode, n_slab, stages, own, below, above, var, miss, out,
    in_b, in_a, picked, whole, sums, work,
    halo_send, halo_recv, mode_send, mode_recv, sum_send, sum_recv,
):
    me = lax.axis_index("mode")
    slab = lax.axis_index("slab")
    mine, count = own.shape
    split = count // n_mode
    n = mine * n_mode
    f = miss.shape[0]
    has_below = slab > 0
    has_above = slab < n_slab - 1
    slab_up = jnp.minimum(slab + 1, n_slab - 1)
    slab_down = jnp.maximum(slab - 1, 0)

    def member(stage, d):
        modes, stride, radix = stage
        low = lax.rem(slab // stride, radix)
        if modes == 1:
            return me, slab + (lax.rem(low + d, radix) - low) * stride
        g = lax.rem(me * radix + low + d, modes * radix)
        return g // radix, slab + (lax.rem(g, radix) - low) * stride

    @pl.when(jnp.logical_not(has_below))
    def _():
        in_b[...] = jnp.zeros_like(in_b)

    @pl.when(jnp.logical_not(has_above))
    def _():
        in_a[...] = jnp.zeros_like(in_a)

    barrier = pltpu.get_barrier_semaphore()

    def greet(device):
        pl.semaphore_signal(barrier, inc=1, device_id=device, device_id_type=pl.DeviceIdType.MESH)

    @pl.when(has_above)
    def _():
        greet((me, slab_up))

    @pl.when(has_below)
    def _():
        greet((me, slab_down))

    greeted = 0
    for d in range(1, n_mode):
        greet((lax.rem(me + d, n_mode), slab))
        greeted += 1
    for stage in stages:
        for d in range(1, stage[0] * stage[2]):
            greet(member(stage, d))
            greeted += 1
    ends = jnp.where(has_below, 1, 0) + jnp.where(has_above, 1, 0)
    pl.semaphore_wait(barrier, greeted + ends)

    def remote(src, dst, send, recv, device):
        return pltpu.make_async_remote_copy(
            src_ref=src, dst_ref=dst, send_sem=send, recv_sem=recv,
            device_id=device, device_id_type=pl.DeviceIdType.MESH,
        )

    pieces = []
    for d in range(n_mode):
        to = lax.rem(me + d, n_mode)
        pieces.append(pl.ds(pl.multiple_of(to * split, 128), split))
    going_up = [
        remote(above.at[:, p], in_b.at[:, p], halo_send.at[d], halo_recv.at[d], (me, slab_up))
        for d, p in enumerate(pieces)
    ]
    going_down = [
        remote(below.at[:, p], in_a.at[:, p], halo_send.at[n_mode + d], halo_recv.at[n_mode + d],
               (me, slab_down))
        for d, p in enumerate(pieces)
    ]
    order = list(range(1, n_mode)) + [0]
    for d in order:

        @pl.when(has_above)
        def _(d=d):
            going_up[d].start()

        @pl.when(has_below)
        def _(d=d):
            going_down[d].start()

    copies = []
    for d in order:

        @pl.when(has_below)
        def _(d=d):
            going_up[d].wait_recv()

        @pl.when(has_above)
        def _(d=d):
            going_down[d].wait_recv()

        p = pieces[d]
        total = own[:, p] + in_b[:, p] + in_a[:, p]
        if d:
            picked[:, p] = total
            to = lax.rem(me + d, n_mode)
            copies.append(
                remote(picked.at[:, p], whole.at[me], mode_send.at[d], mode_recv.at[d], (to, slab))
            )
            copies[-1].start()
        else:
            whole[me] = total
    here = pieces[0]
    for copy in copies:
        copy.wait_recv()
    every = whole[...].reshape(n, split)
    scaled = every / var[:, here]
    gram = lax.dot_general(
        scaled, every, (((1,), (1,)), ((), ())), precision=lax.Precision.HIGHEST,
        preferred_element_type=jnp.float32,
    )
    rhs = lax.dot_general(
        miss[:, here], scaled, (((1,), (1,)), ((), ())), precision=lax.Precision.HIGHEST,
        preferred_element_type=jnp.float32,
    )
    top, some = n // 2, f // 2
    sums[0, :top, :n] = gram[:top]
    sums[0, :top, n:] = gram[top:]
    sums[0, top:, :n] = rhs[:some]
    sums[0, top:, n:] = rhs[some:]

    base = 0
    sem = 0
    for stage in stages:
        size = stage[0] * stage[2]
        if base:
            sums[base] = total
        moving = []
        for d in range(1, size):
            moving.append(
                remote(sums.at[base], sums.at[base + d], sum_send.at[sem], sum_recv.at[sem],
                       member(stage, d))
            )
            moving[-1].start()
            sem += 1
        low = lax.rem(slab // stage[1], stage[2])
        if stage[0] > 1:
            low = low + me * stage[2]
        for copy in moving:
            copy.wait_recv()
        total = None
        for q in range(size):
            term = sums[base + lax.rem(low - q + size, size)]
            total = term if total is None else total + term
        copies += moving
        base += size

    work[...] = jnp.zeros_like(work)
    work[:top, :n] = total[:top, :n]
    work[top:n, :n] = total[:top, n:]
    work[n : n + some, :n] = total[top:, :n]
    work[n + some : n + f, :n] = total[top:, n:]
    matrix = work[...].T[:n]
    tall = lax.broadcasted_iota(jnp.int32, matrix.shape, 0)
    wide = lax.broadcasted_iota(jnp.int32, matrix.shape, 1)
    work[:n] = eliminate(matrix + jnp.where(tall == wide, 1.0, 0.0), n)
    for d in range(n_mode):
        block = lax.rem(me - d + n_mode, n_mode)
        out[d * mine : (d + 1) * mine, :] = work[
            pl.ds(pl.multiple_of(block * mine, 8), mine), n : n + f
        ]

    @pl.when(has_above)
    def _():
        for copy in going_up:
            copy.wait_send()

    @pl.when(has_below)
    def _():
        for copy in going_down:
            copy.wait_send()

    for copy in copies:
        copy.wait_send()


def reduce_and_solve(own, below, above, obs_var, misfit):
    n_mode = lax.axis_size("mode")
    n_slab = lax.axis_size("slab")
    mine, count = own.shape
    n = mine * n_mode
    f = misfit.shape[1]
    stages = stages_of(n_mode, n_slab)
    slots = sum(s[0] * s[2] for s in stages)
    wide = 128 * pl.cdiv(n + f, 128)
    vmem = pl.BlockSpec(memory_space=pltpu.VMEM)
    dma = pltpu.SemaphoreType.DMA
    return pl.pallas_call(
        functools.partial(reduce_kernel, n_mode, n_slab, stages),
        out_shape=jax.ShapeDtypeStruct((n, f), jnp.float32),
        in_specs=[vmem] * 5,
        out_specs=vmem,
        scratch_shapes=[
            pltpu.VMEM((mine, count), jnp.float32),
            pltpu.VMEM((mine, count), jnp.float32),
            pltpu.VMEM((mine, count), jnp.float32),
            pltpu.VMEM((n_mode, mine, count // n_mode), jnp.float32),
            pltpu.VMEM((slots, (n + f) // 2, 2 * n), jnp.float32),
            pltpu.VMEM((wide, wide), jnp.float32),
            dma((2 * n_mode,)), dma((2 * n_mode,)), dma((n_mode,)), dma((n_mode,)), dma((slots,)), dma((slots,)),
        ],
        compiler_params=pltpu.CompilerParams(
            collective_id=0, has_side_effects=True, vmem_limit_bytes=24 * MIB
        ),
        cost_estimate=pl.CostEstimate(
            flops=2 * n * n * count, bytes_accessed=1 << 20, transcendentals=0
        ),
        name="reduce_and_solve",
    )(own, below, above, obs_var.reshape(1, count), misfit.T)


def update_kernel(place_ref, coef_ref, own_ref, others_ref, base_ref, out_ref, big):
    fields, deep, rows, lanes = out_ref.shape
    total = coef_ref.shape[0]
    mine = own_ref.shape[0]

    @pl.when(jnp.logical_and(pl.program_id(0) == 0, pl.program_id(1) == 0))
    def _():
        coef = coef_ref[...]
        high = coef.astype(jnp.bfloat16)
        low = (coef - high.astype(jnp.float32)).astype(jnp.bfloat16)
        tall, wide = fields * ROWS, total * ROWS
        r0 = lax.broadcasted_iota(jnp.int32, (tall, fields), 0)
        f0 = lax.broadcasted_iota(jnp.int32, (tall, fields), 1)
        spread_f = jnp.where(r0 // ROWS == f0, 1.0, 0.0).astype(jnp.bfloat16)
        k0 = lax.broadcasted_iota(jnp.int32, (total, wide), 0)
        c0 = lax.broadcasted_iota(jnp.int32, (total, wide), 1)
        spread_k = jnp.where(c0 // ROWS == k0, 1.0, 0.0).astype(jnp.bfloat16)
        r1 = lax.broadcasted_iota(jnp.int32, (tall, wide), 0)
        c1 = lax.broadcasted_iota(jnp.int32, (tall, wide), 1)
        same = r1 % ROWS == c1 % ROWS
        for p, part in enumerate((high, low)):
            a = lax.dot_general(
                spread_f, part, (((1,), (1,)), ((), ())), preferred_element_type=jnp.float32
            ).astype(jnp.bfloat16)
            b = jnp.dot(a, spread_k, preferred_element_type=jnp.float32)
            big[p * tall : (p + 1) * tall, :] = jnp.where(same, b, 0.0).astype(jnp.bfloat16)

    tall = fields * ROWS
    left = mine * ROWS

    def side(ref):
        count = ref.shape[0]
        tiles = []
        for d in range(deep):
            whole = ref[:, d].astype(jnp.float32)
            for h in range(rows // ROWS):
                tile = whole[:, h * ROWS : (h + 1) * ROWS, :]
                tiles.append(tile.reshape(count * ROWS, lanes).astype(jnp.bfloat16))
        return jnp.concatenate(tiles, axis=1)

    both = jnp.dot(big[:, :left], side(own_ref), preferred_element_type=jnp.float32)
    both = both + jnp.dot(big[:, left:], side(others_ref), preferred_element_type=jnp.float32)
    both = both[:tall] + both[tall:]
    for d in range(deep):
        base = base_ref[:, d].astype(jnp.float32)
        for h in range(rows // ROWS):
            at = (d * (rows // ROWS) + h) * lanes
            part = both[:, at : at + lanes].reshape(fields, ROWS, lanes)
            out_ref[:, d, h * ROWS : (h + 1) * ROWS, :] = (
                base[:, h * ROWS : (h + 1) * ROWS, :] + part
            )


def update(place, coef, modes, others, base):
    fields, planes, width, lanes = base.shape
    mine = modes.shape[0]
    rest = others.shape[0]
    rows = 16
    deep = 2
    steps = width // rows

    def fixed(count):
        return pl.BlockSpec((count, deep, rows, lanes), lambda z, x, place: (0, z, x, 0))

    return pl.pallas_call(
        update_kernel,
        grid_spec=pltpu.PrefetchScalarGridSpec(
            num_scalar_prefetch=1,
            grid=(planes // deep, steps),
            in_specs=[
                pl.BlockSpec(coef.shape, lambda z, x, place: (0, 0)),
                pl.BlockSpec(
                    (mine, deep, rows, lanes),
                    lambda z, x, place: (0, z, place[0] * steps + x, 0),
                ),
                fixed(rest),
                fixed(fields),
            ],
            out_specs=fixed(fields),
            scratch_shapes=[
                pltpu.VMEM((2 * fields * ROWS, (mine + rest) * ROWS), jnp.bfloat16)
            ],
        ),
        out_shape=jax.ShapeDtypeStruct(base.shape, jnp.float32),
        compiler_params=pltpu.CompilerParams(
            dimension_semantics=("arbitrary", "arbitrary"), vmem_limit_bytes=32 * MIB
        ),
        name="update",
    )(place, coef, modes, others, base)


def on_device(log_cond, head_slope, modes, obs_cells, obs_var, misfit, base_fields):
    n_mode = lax.axis_size("mode")
    me = lax.axis_index("mode")
    log_ext, plan, *pieces = halo(log_cond, obs_cells, modes)
    received = [
        lax.ppermute(piece, "mode", [(i, (i + d) % n_mode) for i in range(n_mode)])
        for d, piece in enumerate(pieces, 1)
    ]
    others = received[0] if n_mode == 2 else jnp.concatenate(received, axis=0)
    own, below, above = stencil(plan, log_ext, head_slope, modes)
    coef = reduce_and_solve(own, below, above, obs_var, misfit)
    return update(me.astype(jnp.int32).reshape(1), coef, modes, others, base_fields)


def solution(mesh):
    placed = (
        P("slab", None, None),
        P("slab", None, None),
        P("mode", "slab", None, None),
        P("slab"),
        P("slab"),
        P("slab", None),
        P(None, "slab", "mode", None),
    )
    return jax.shard_map(
        on_device,
        mesh=mesh,
        in_specs=placed,
        out_specs=P(None, "slab", "mode", None),
        check_vma=False,
    )
```
